32 devices in a mesh: lag: 4 (over y, core), col: 8 (over z, x).
Axes of the slice: x: 2, y: 2, z: 4, core: 2. Of those that a mesh axis runs over, the one named last changes fastest.
Arguments:
- lag_matrices: float32 [64, 2048, 2048], P('lag', None, 'col'), may hold values from -0.03125 to 0.03125
- history: float32 [64, 2048, 256], P('lag', 'col'), may hold values from -6 to 6
- excitation: float32 [4, 2048, 256], P(None, 'col'), may hold values from -6 to 6
Outputs:
- densities: float32 [4, 2048, 256], P(None, 'col')
The draws below stay inside these ranges and needn't reach their ends.
All inputs are finite; a program needn't handle non-finite values.
Results may differ from the reference program's by a relative error of at most 0.0001.
Values sent between devices are 32-bit elements; how exact they have to be, the bound alone decides.
No kernel may reach another device: no remote copies, remote signals or barrier semaphores. Data moves between devices by JAX's collectives and lax.ppermute only.
A program may use at most 128 MiB of HBM per device.

```python
import jax
import jax.numpy as jnp
from jax import lax

U = 2048
R = 256
STEPS = 4
LAGS = 64


def with_spikes(drawn, stream_key, source, target, shards_of, factor):
    def block_of(dim):
        return (jnp.arange(drawn.shape[dim]) // (drawn.shape[dim] // shards_of)).reshape((-1,) + (1,) * (drawn.ndim - 1 - dim))

    one_side = jax.random.permutation(stream_key, shards_of)[block_of(target)]
    far = (block_of(target) + shards_of // 2) % shards_of
    return jnp.where((block_of(source) == one_side) | (block_of(source) == far), factor * drawn, drawn)


def shard_levels(own_key, extent, pieces, low, largest):
    factor_of, own = 1.0, jax.random.fold_in(own_key, 6)
    for dim, parts in pieces:
        heights = jnp.exp(jax.random.uniform(jax.random.fold_in(own, dim), (parts,), jnp.float32, low / len(pieces), largest / len(pieces)))
        factor_of = factor_of * jnp.repeat(heights, extent[dim] // parts).reshape([-1 if axis == dim else 1 for axis in range(len(extent))])
    return factor_of


def normal_values(rng, shape, scale, bound, cuts=(), held_as=jnp.bfloat16):
    gain = shard_levels(rng, shape, cuts, -0.22, 0.18) if cuts else 1.0
    result = jax.random.normal(rng, shape, jnp.float32) * scale * gain
    return jnp.minimum(jnp.maximum(result, -bound), bound).astype(held_as)


def gaussian_with(stream_key, extent, scale, most, cuts, heavy, kind=jnp.bfloat16):
    result = scale * jax.random.normal(stream_key, extent, jnp.float32)
    if cuts:
        result = result * shard_levels(stream_key, extent, cuts, -0.22, 0.18)
    return jnp.clip(with_spikes(result, jax.random.fold_in(stream_key, 3), *heavy), -most, most).astype(kind)


def setup_inputs(seed: int = 0) -> dict:
    seeds = jax.random.split(jax.random.key(seed), 4)
    return {
        "lag_matrices": gaussian_with(seeds[0], (LAGS, U, U), (40 * U) ** -0.5, 0.03125, ((0, 4), (2, 8)), (2, 1, 8, 2.0), jnp.float32),
        "history": normal_values(seeds[1], (LAGS, U, R), 1.0, 6.0, ((0, 4), (1, 8)), jnp.float32),
        "excitation": normal_values(seeds[2], (STEPS, U, R), 1.0, 6.0, ((1, 8),), jnp.float32),
    }


def reference(lag_matrices, history, excitation):
    densities = []
    for moment in range(STEPS):
        if moment > 0:
            recent = jnp.stack([densities[moment - 1 - offset] for offset in range(moment)])
            stacked = jnp.concatenate([recent, history[:LAGS - moment]], axis=0)
        else:
            stacked = history
        total = jnp.einsum("kab,kbr->ar", lag_matrices, stacked, precision=lax.Precision.HIGHEST)
        densities.append(excitation[moment] - total)
    return jnp.stack(densities)
```

```python
import functools

import jax
import jax.numpy as jnp
from jax import lax
from jax.experimental import pallas as pl
from jax.experimental.pallas import tpu as pltpu
from jax.sharding import PartitionSpec as P

LANES = 128
BF = jnp.bfloat16
F32 = jnp.float32
FIRST = ((1, 1), (1, 2), (2, 1), (2, 2))
REST = ((1, 3), (2, 3), (3, 1), (3, 2), (3, 3))
MEMBERS = {1: (1,), 2: (0, 1), 3: (0,)}


def swap_pairs(axis, bit):
    return [(i, i ^ bit) for i in range(lax.axis_size(axis))]


def exchanged(value, axis, bit):
    return lax.ppermute(value, axis, swap_pairs(axis, bit))


def bit_count(n):
    return n.bit_length() - 1


def reversed_bits(n):
    bits = bit_count(n)
    return [sum(((i >> b) & 1) << (bits - 1 - b) for b in range(bits)) for i in range(n)]


def split(v):
    hi = v.astype(BF)
    return hi, (v - hi.astype(F32)).astype(BF)


def dot(a, b):
    return jnp.dot(a, b, preferred_element_type=F32)


def flipped(v, own, slices):
    cols = v.shape[-1]
    width = cols // slices
    for b in range(bit_count(slices)):
        step = width << b
        swapped = jnp.concatenate(
            [v[:, (start ^ step) : (start ^ step) + step] for start in range(0, cols, step)], axis=1
        )
        v = jnp.where(((own >> b) & 1) == 1, swapped, v)
    return v


def folded(v):
    rows, width = v.shape
    parts = LANES // width
    step = rows // parts
    return jnp.concatenate([v[s * step : (s + 1) * step] for s in range(parts)], axis=1) if parts > 1 else v


def unfolded(v, width):
    parts = LANES // width
    return jnp.concatenate([v[:, s * width : (s + 1) * width] for s in range(parts)], axis=0) if parts > 1 else v


def write_folded(y, block, keep_ref, send_ref, slices):
    width = y.shape[1] // slices
    small = block * width // LANES
    order = reversed_bits(slices)
    half = slices // 2
    for b in range(y.shape[0] // block):
        rows = y[b * block : (b + 1) * block]
        for i, p in enumerate(order):
            piece = folded(rows[:, p * width : (p + 1) * width])
            ref = keep_ref if i < half else send_ref
            ref[i % half, b * small : (b + 1) * small, :] = piece


def source_sums(get, outer, inner, base):
    def along(inner_offset):
        if outer == 1:
            return get(base + 2 + inner_offset) - get(base + inner_offset)
        if outer == 2:
            return get(base + inner_offset)
        return get(base + inner_offset) - get(base - 2 + inner_offset)

    if inner == 1:
        return along(1) - along(0)
    if inner == 2:
        return along(0)
    return along(0) - along(-1)


def prepare_sources(kinds, get, own, slices, groups, hi_ref, lo_ref):
    block = hi_ref.shape[1] // groups
    for i, (outer, inner) in enumerate(kinds):
        for g in range(groups):
            hi, lo = split(flipped(source_sums(get, outer, inner, 4 * g), own, slices))
            hi_ref[i, g * block : (g + 1) * block, :] = hi
            lo_ref[i, g * block : (g + 1) * block, :] = lo


def products(kinds, a_ref, hi_ref, lo_ref):
    groups = a_ref.shape[0] // 4
    out = []
    for i, (outer, inner) in enumerate(kinds):
        his, los = [], []
        for g in range(groups):
            total = None
            for u in MEMBERS[outer]:
                for v in MEMBERS[inner]:
                    term = a_ref[4 * g + 2 * u + v]
                    total = term if total is None else total + term
            hi, lo = split(total)
            his.append(hi)
            los.append(lo)
        hi, lo = jnp.concatenate(his, axis=1), jnp.concatenate(los, axis=1)
        out.append(dot(hi, hi_ref[i]) + dot(hi, lo_ref[i]) + dot(lo, hi_ref[i]))
    return out


def first_kernel(own_ref, history_ref, a_ref, keep_ref, send_ref, q1_ref, q2_ref, q3_ref, hi_ref, lo_ref, *, slices, block):
    groups = a_ref.shape[0] // 4

    @pl.when(pl.program_id(0) == 0)
    def _():
        prepare_sources(FIRST, lambda i: history_ref[i], own_ref[0], slices, groups, hi_ref, lo_ref)

    p11, p12, p21, p22 = products(FIRST, a_ref, hi_ref, lo_ref)
    q1 = p12 + p22
    q1_ref[...] = q1
    q2_ref[...] = p21 + p22
    q3_ref[...] = p22
    write_folded(q1 + (p11 + p21), block, keep_ref, send_ref, slices)


def rest_kernel(own_ref, history_ref, carried_ref, a_ref, q1_ref, q2_ref, q3_ref, *refs, slices, block):
    outs, (hi_ref, lo_ref) = refs[:-2], refs[-2:]
    groups = a_ref.shape[0] // 4
    back = carried_ref.shape[0]

    @pl.when(pl.program_id(0) == 0)
    def _():
        def get(i):
            return history_ref[i] if i >= 0 else carried_ref[back + i]

        prepare_sources(REST, get, own_ref[0], slices, groups, hi_ref, lo_ref)

    p13, p23, p31, p32, p33 = products(REST, a_ref, hi_ref, lo_ref)
    y1 = q1_ref[...] - (p13 + p23)
    y2 = q2_ref[...] - (p31 + p32)
    y3 = (q3_ref[...] - p23) - (p32 - p33)
    for n, y in enumerate((y1, y2, y3)):
        write_folded(y, block, outs[2 * n], outs[2 * n + 1], slices)


def smem():
    return pl.BlockSpec(memory_space=pltpu.SMEM)


def bulk(kernel, name, kinds, own, whole, matrices, partials, steps, slices, tile):
    lags, rows, block = matrices.shape
    cols = whole[0].shape[2]
    groups = lags // 4
    small = tile * (cols // slices) // LANES
    flat = jax.ShapeDtypeStruct((slices // 2, rows * (cols // slices) // LANES, LANES), F32)
    flat_spec = pl.BlockSpec((slices // 2, small, LANES), lambda i: (0, i, 0))
    row_spec = pl.BlockSpec((tile, cols), lambda i: (i, 0))
    saved = 0 if partials else 3
    return pl.pallas_call(
        functools.partial(kernel, slices=slices, block=block),
        grid=(rows // tile,),
        in_specs=[smem()]
        + [pl.BlockSpec(w.shape, lambda i: (0, 0, 0)) for w in whole]
        + [pl.BlockSpec((lags, tile, block), lambda i: (0, i, 0))]
        + [row_spec] * len(partials),
        out_specs=[flat_spec] * (2 * steps) + [row_spec] * saved,
        out_shape=[flat] * (2 * steps) + [jax.ShapeDtypeStruct((rows, cols), F32)] * saved,
        scratch_shapes=[pltpu.VMEM((len(kinds), groups * block, cols), BF)] * 2,
        compiler_params=pltpu.CompilerParams(vmem_limit_bytes=56 << 20),
        cost_estimate=pl.CostEstimate(
            flops=2 * 3 * len(kinds) * groups * rows * block * cols,
            bytes_accessed=4 * (matrices.size + 4 * rows * cols),
            transcendentals=0,
        ),
        name=name,
    )(own, *whole, matrices, *partials)


def merge_kernel(own_ref, a_ref, b_ref, keep_ref, send_ref):
    own = own_ref[0]
    for q in range(a_ref.shape[0]):
        c = own ^ q
        (send_ref if q % 2 else keep_ref)[q // 2] = a_ref[c] + b_ref[c]


def chain_kernel(own_ref, e_ref, a_ref, b_ref, m_ref, *refs, width):
    parts, (x_ref, keep_ref, send_ref) = refs[:-3], refs[-3:]
    own = own_ref[0]
    total = parts[0][...]
    for part in parts[1:]:
        total = total + part[...]
    x = e_ref[...] - total
    x_ref[...] = x
    block = m_ref.shape[1]
    x_hi, x_lo = split(unfolded(x, width))
    x_both = jnp.concatenate([x_hi, x_lo], axis=1)
    for q in range(a_ref.shape[0]):
        c = own ^ q
        m_hi, m_lo = split(m_ref[pl.ds(pl.multiple_of(c * block, block), block), :])
        both = dot(m_hi, x_both)
        y = both[:, :width] + both[:, width:] + dot(m_lo, x_hi)
        (send_ref if q % 2 else keep_ref)[q // 2] = folded(y) + (a_ref[c] + b_ref[c])


def late_kernel(own_ref, acc_ref, *refs, width, owners):
    out_ref, pairs = refs[-1], refs[:-1]
    half, rows, _ = acc_ref.shape

    @pl.when(own_ref[0] >= owners)
    def _():
        out_ref[...] = acc_ref[...]

    @pl.when(own_ref[0] < owners)
    def _():
        block = pairs[0].shape[1]
        small = block * width // LANES
        sources = []
        for i in range(0, len(pairs), 2):
            x = jnp.concatenate([unfolded(pairs[i + 1][p], width) for p in range(half)], axis=1)
            sources.append(split(x))
        for c in range(pairs[0].shape[0] // block):
            y = None
            for i, (x_hi, x_lo) in enumerate(sources):
                m_hi, m_lo = split(pairs[2 * i][c * block : (c + 1) * block, :])
                term = dot(m_hi, x_hi) + dot(m_hi, x_lo) + dot(m_lo, x_hi)
                y = term if y is None else y + term
            for p in range(half):
                at = (p, slice(c * small, (c + 1) * small))
                out_ref[at] = acc_ref[at] + folded(y[:, p * width : (p + 1) * width])


def fields_kernel(own_ref, e_ref, out_ref, *, slices):
    width = e_ref.shape[2] // slices
    for n in range(e_ref.shape[0]):
        out_ref[n] = folded(flipped(e_ref[n], own_ref[0], slices)[:, :width])


def assemble_kernel(own_ref, parts_ref, out_ref, *, slices):
    width = out_ref.shape[2] // slices
    order = reversed_bits(slices)
    for n in range(out_ref.shape[0]):
        pieces = [None] * slices
        for i, p in enumerate(order):
            pieces[p] = unfolded(parts_ref[i, n], width)
        out_ref[n] = flipped(jnp.concatenate(pieces, axis=1), own_ref[0], slices)


def whole_call(kernel, name, out_shapes, *args):
    vmem = pl.BlockSpec(memory_space=pltpu.VMEM)
    out = [jax.ShapeDtypeStruct(s, F32) for s in out_shapes]
    return pl.pallas_call(
        kernel,
        in_specs=[smem()] + [vmem] * (len(args) - 1),
        out_specs=[vmem] * len(out),
        out_shape=out,
        compiler_params=pltpu.CompilerParams(vmem_limit_bytes=40 << 20),
        name=name,
    )(*args)


def local(lag_matrices, history, excitation):
    owners, columns = lax.axis_size("lag"), lax.axis_size("col")
    owner, column = lax.axis_index("lag"), lax.axis_index("col")
    lags, rows, block = lag_matrices.shape
    steps, _, cols = excitation.shape
    width = cols // owners
    small = block * width // LANES
    bits = bit_count(owners)
    back = steps - 1
    own_lag = jnp.reshape(owner, (1,)).astype(jnp.int32)
    own_col = jnp.reshape(column, (1,)).astype(jnp.int32)
    tile = min(rows, 512)

    carried = lax.ppermute(history[lags - back :], "lag", [(i, i + 1) for i in range(owners - 1)])

    newest = lag_matrices[0]
    for b in reversed(range(1, bits)):
        pairs = [(i, i + (1 << b)) for i in range(0, owners, 2 << b)]
        got = lax.ppermute(newest, "lag", pairs)
        newest = jnp.where((owner >> b) & 1 == 1, got, newest)
    got = lax.ppermute(newest, "lag", [(i, i + 1) for i in range(0, owners, 2)])
    newest = jnp.where(owner & 1 == 1, got, newest)
    older = lag_matrices[1:back]
    got = lax.ppermute(older, "lag", [(0, 1)])
    older = jnp.where(owner & 1 == 1, got, older)

    field = whole_call(functools.partial(fields_kernel, slices=owners), "fields", [(steps, small, LANES)], own_lag, excitation)[0]
    keep0, send0, q1, q2, q3 = bulk(first_kernel, "first", FIRST, own_lag, [history], lag_matrices, [], 1, owners, tile)
    rest = bulk(rest_kernel, "rest", REST, own_lag, [history, carried], lag_matrices, [q1, q2, q3], back, owners, tile)
    keeps = [keep0, *rest[0::2]]
    sends = [send0, *rest[1::2]]

    def own_sums(n, gathered):
        acc = keeps[n] + exchanged(sends[n], "lag", 1)
        if n >= 2:
            args = []
            for k in range(2, n + 1):
                args += [older[k - 2], gathered[n - k]]
            acc = whole_call(functools.partial(late_kernel, width=width, owners=2), "late", [acc.shape], own_lag, acc, *args)[0]
        for b in range(1, bits):
            half = acc.shape[0] // 2
            got = exchanged(acc[half:], "lag", 1 << b)
            if half == 1:
                return acc[0], got[0]
            acc = acc[:half] + got
        return acc[0], jnp.zeros_like(acc[0])

    def scattered(keep, send):
        acc = keep + exchanged(send, "col", 1)
        bit = 2
        while acc.shape[0] > 4:
            got = exchanged(acc[1::2], "col", bit)
            acc = acc[0::2] + got
            bit *= 2
        return [acc[0]] + [exchanged(acc[d], "col", d * bit) for d in range(1, acc.shape[0])]

    halves = [(columns // 2, small, LANES)] * 2
    shaped = (columns, small, LANES)
    found, gathered = [], []
    a, b = own_sums(0, gathered)
    keep, send = whole_call(merge_kernel, "merge", halves, own_col, a.reshape(shaped), b.reshape(shaped))
    for n in range(1, steps):
        parts = scattered(keep, send)
        a, b = own_sums(n, gathered)
        x, keep, send = whole_call(
            functools.partial(chain_kernel, width=width), "chain", [(small, LANES), *halves],
            own_col, field[n - 1], a.reshape(shaped), b.reshape(shaped), newest, *parts,
        )
        found.append(x)
        near = x[None]
        for bit in reversed(range(1, bits)):
            near = jnp.concatenate([near, exchanged(near, "lag", 1 << bit)], axis=0)
        gathered.append(near)
    parts = scattered(keep, send)
    x = field[steps - 1] - functools.reduce(jnp.add, parts)
    near = x[None]
    for bit in reversed(range(1, bits)):
        near = jnp.concatenate([near, exchanged(near, "lag", 1 << bit)], axis=0)
    gathered.append(near)
    every = jnp.stack(gathered, axis=1)
    every = jnp.concatenate([every, exchanged(every, "lag", 1)], axis=0)
    return whole_call(functools.partial(assemble_kernel, slices=owners), "assemble", [excitation.shape], own_lag, every)[0]


def solution(mesh):
    return jax.shard_map(
        local,
        mesh=mesh,
        in_specs=(P("lag", None, "col"), P("lag", "col", None), P(None, "col", None)),
        out_specs=P(None, "col", None),
        check_vma=False,
    )
```

```python
import functools

import jax
import jax.numpy as jnp
from jax import lax
from jax.experimental import pallas as pl
from jax.experimental.pallas import tpu as pltpu
from jax.sharding import PartitionSpec as P

LANES = 128
BF = jnp.bfloat16
F32 = jnp.float32
LIGHT = pl.CostEstimate(flops=1, bytes_accessed=1, transcendentals=0)
KINDS = tuple((outer, inner) for outer in (1, 2, 3) for inner in (1, 2, 3))
MEMBERS = {1: (1,), 2: (0, 1), 3: (0,)}


def swap_pairs(axis, bit):
    return [(i, i ^ bit) for i in range(lax.axis_size(axis))]


def exchanged(value, axis, bit):
    return lax.ppermute(value, axis, swap_pairs(axis, bit))


def bit_count(n):
    return n.bit_length() - 1


def reversed_bits(n):
    bits = bit_count(n)
    return [sum(((i >> b) & 1) << (bits - 1 - b) for b in range(bits)) for i in range(n)]


def split(v):
    hi = v.astype(BF)
    return hi, (v - hi.astype(F32)).astype(BF)


def dot(a, b):
    return jnp.dot(a, b, preferred_element_type=F32)


def flipped(v, own, slices):
    cols = v.shape[-1]
    width = cols // slices
    for b in range(bit_count(slices)):
        step = width << b
        swapped = jnp.concatenate(
            [v[:, (start ^ step) : (start ^ step) + step] for start in range(0, cols, step)], axis=1
        )
        v = jnp.where(((own >> b) & 1) == 1, swapped, v)
    return v


def folded(v):
    rows, width = v.shape
    parts = LANES // width
    step = rows // parts
    return jnp.concatenate([v[s * step : (s + 1) * step] for s in range(parts)], axis=1) if parts > 1 else v


def unfolded(v, width):
    parts = LANES // width
    return jnp.concatenate([v[:, s * width : (s + 1) * width] for s in range(parts)], axis=0) if parts > 1 else v


def source_sums(get, outer, inner, base):
    def along(inner_offset):
        if outer == 1:
            return get(base + 2 + inner_offset) - get(base + inner_offset)
        if outer == 2:
            return get(base + inner_offset)
        return get(base + inner_offset) - get(base - 2 + inner_offset)

    if inner == 1:
        return along(1) - along(0)
    if inner == 2:
        return along(0)
    return along(0) - along(-1)


def prepare_sources(kinds, get, own, slices, groups, hi_ref, lo_ref):
    block = hi_ref.shape[1] // groups
    for i, (outer, inner) in enumerate(kinds):
        for g in range(groups):
            hi, lo = split(flipped(source_sums(get, outer, inner, 4 * g), own, slices))
            hi_ref[i, g * block : (g + 1) * block, :] = hi
            lo_ref[i, g * block : (g + 1) * block, :] = lo


def write_folded(y, block, keep_ref, send_ref, slices):
    width = y.shape[1] // slices
    small = block * width // LANES
    half = slices // 2
    for b in range(y.shape[0] // block):
        rows = y[b * block : (b + 1) * block]
        for i, p in enumerate(reversed_bits(slices)):
            piece = folded(rows[:, p * width : (p + 1) * width])
            (send_ref if i // half else keep_ref)[i % half, b * small : (b + 1) * small, :] = piece


def slot(core, x_part, y_part, half):
    top, low = y_part // (half // 2), y_part % (half // 2)
    return jnp.where(core == 0, (x_part * 2 + top) * (half // 2) + low, (top * 2 + x_part) * (half // 2) + low)


def write_slots(y, block, own_ref, keep_ref, send_ref, slices):
    width = y.shape[1] // slices
    half = slices // 2
    core, side = own_ref[0] & 1, own_ref[1] & 1
    for b in range(y.shape[0] // block):
        rows = y[b * block : (b + 1) * block]
        for i, p in enumerate(reversed_bits(slices)):
            piece = folded(rows[:, p * width : (p + 1) * width])
            at = slot(core ^ (i // half), (b & 1) ^ side, i % half, half)
            (send_ref if i // half else keep_ref)[at, b // 2, :, :] = piece


def products(kinds, a_ref, hi_ref, lo_ref):
    groups = a_ref.shape[0]
    out = []
    for i, (outer, inner) in enumerate(kinds):
        his, los = [], []
        for g in range(groups):
            total = None
            for u in MEMBERS[outer]:
                for v in MEMBERS[inner]:
                    term = a_ref[g, u, v]
                    total = term if total is None else total + term
            hi, lo = split(total)
            his.append(hi)
            los.append(lo)
        hi, lo = jnp.concatenate(his, axis=1), jnp.concatenate(los, axis=1)
        out.append(dot(hi, hi_ref[i]) + dot(hi, lo_ref[i]) + dot(lo, hi_ref[i]))
    return out


def bulk_kernel(own_ref, history_ref, a_ref, *refs, slices, block):
    outs, (second_ref, third_ref, hi_ref, lo_ref) = refs[:-4], refs[-4:]

    @pl.when(pl.program_id(0) == 0)
    def _():
        def get(i):
            return history_ref[i] if i >= 0 else jnp.zeros(history_ref.shape[1:], F32)

        prepare_sources(KINDS, get, own_ref[0], slices, a_ref.shape[0], hi_ref, lo_ref)

    second_ref[...] = a_ref[0, 0, 1]
    third_ref[...] = a_ref[0, 1, 0]
    p11, p12, p13, p21, p22, p23, p31, p32, p33 = products(KINDS, a_ref, hi_ref, lo_ref)
    write_slots((p12 + p22) + (p11 + p21), block, own_ref, outs[0], outs[1], slices)
    times = ((p12 + p22) - (p13 + p23), (p21 + p22) - (p31 + p32), (p22 - p23) - (p32 - p33))
    for n, y in enumerate(times):
        write_folded(y, block, outs[2 * n + 2], outs[2 * n + 3], slices)


def carried_kernel(own_ref, tail_ref, keep_in, send_in, *refs, slices):
    matrices, (keep_ref, send_ref) = refs[:-2], refs[-2:]
    back, block = tail_ref.shape[:2]
    count = len(matrices)
    width = tail_ref.shape[2] // slices
    small = block * width // LANES
    half = slices // 2
    x = jnp.concatenate([flipped(tail_ref[back - count + j], own_ref[0], slices) for j in range(count)], axis=0)
    x_hi, x_lo = split(x)
    for c in range(matrices[0].shape[1] // block):
        m_hi, m_lo = split(jnp.concatenate([r[0, c * block : (c + 1) * block, :] for r in matrices], axis=1))
        y = dot(m_hi, x_hi) + dot(m_hi, x_lo) + dot(m_lo, x_hi)
        for i, p in enumerate(reversed_bits(slices)):
            at = (i % half, slice(c * small, (c + 1) * small))
            from_ref, to_ref = (send_in, send_ref) if i // half else (keep_in, keep_ref)
            to_ref[at] = from_ref[at] + folded(y[:, p * width : (p + 1) * width])


def with_carried(own, tail, keep, send, matrices, count, slices):
    lags, rows, block = matrices.shape
    return pl.pallas_call(
        functools.partial(carried_kernel, slices=slices),
        grid=(1,),
        in_specs=[smem()]
        + [pl.BlockSpec(v.shape, lambda i: (0, 0, 0)) for v in (tail, keep, send)]
        + [pl.BlockSpec((1, rows, block), lambda i, j=j: (j, 0, 0)) for j in range(count)],
        out_specs=[pl.BlockSpec(keep.shape, lambda i: (0, 0, 0))] * 2,
        out_shape=[jax.ShapeDtypeStruct(keep.shape, F32)] * 2,
        compiler_params=pltpu.CompilerParams(vmem_limit_bytes=40 << 20),
        cost_estimate=LIGHT,
        name="carried",
    )(own, tail, keep, send, *[matrices] * count)


def smem():
    return pl.BlockSpec(memory_space=pltpu.SMEM)


def bulk(own, history, matrices, steps, slices, tiles):
    lags, rows, block = matrices.shape
    cols = history.shape[2]
    groups = lags // 4
    tile = rows // tiles
    small = block * (cols // slices) // LANES
    pairs = rows // block // 2
    flat = jax.ShapeDtypeStruct((slices // 2, 2 * pairs * small, LANES), F32)
    flat_spec = pl.BlockSpec((slices // 2, 2 * pairs * small // tiles, LANES), lambda i: (0, i, 0))
    slots = jax.ShapeDtypeStruct((slices, pairs, small, LANES), F32)
    slots_spec = pl.BlockSpec((slices, pairs // tiles, small, LANES), lambda i: (0, i, 0, 0))
    return pl.pallas_call(
        functools.partial(bulk_kernel, slices=slices, block=block),
        grid=(tiles,),
        in_specs=[
            smem(),
            pl.BlockSpec(history.shape, lambda i: (0, 0, 0)),
            pl.BlockSpec((groups, 2, 2, tile, block), lambda i: (0, 0, 0, i, 0)),
        ],
        out_specs=[slots_spec] * 2 + [flat_spec] * (2 * steps - 2) + [pl.BlockSpec((tile, block), lambda i: (i, 0))] * 2,
        out_shape=[slots] * 2 + [flat] * (2 * steps - 2) + [jax.ShapeDtypeStruct((rows, block), F32)] * 2,
        scratch_shapes=[pltpu.VMEM((len(KINDS), groups * block, cols), BF)] * 2,
        compiler_params=pltpu.CompilerParams(vmem_limit_bytes=61 << 20),
        cost_estimate=pl.CostEstimate(
            flops=2 * 4 * len(KINDS) * groups * rows * block * cols,
            bytes_accessed=4 * matrices.size,
            transcendentals=0,
        ),
        name="bulk",
    )(own, history, matrices.reshape(groups, 2, 2, rows, block))


def stage_kernel(own_ref, a_ref, *refs):
    slabs, (newest_ref, tail_ref) = refs[:-2], refs[-2:]
    newest_ref[...] = a_ref[0]
    for i, slab in enumerate(slabs):
        tail_ref[i] = slab[0]


def staged(own, matrices, history, back):
    lags, rows, block = matrices.shape
    cols = history.shape[2]
    shapes = [(rows, block), (back, block, cols)]
    return pl.pallas_call(
        stage_kernel,
        grid=(1,),
        in_specs=[smem(), pl.BlockSpec((1, rows, block), lambda i: (0, 0, 0))]
        + [pl.BlockSpec((1, block, cols), lambda i, at=lags - back + k: (at, 0, 0)) for k in range(back)],
        out_specs=[pl.BlockSpec(s, lambda i, r=len(s): (0,) * r) for s in shapes],
        out_shape=[jax.ShapeDtypeStruct(s, F32) for s in shapes],
        compiler_params=pltpu.CompilerParams(vmem_limit_bytes=61 << 20),
        cost_estimate=LIGHT,
        name="stage",
    )(own, matrices, *[history] * back)


def merge_kernel(own_ref, a_ref, *out_refs):
    for d, out_ref in enumerate(out_refs):
        out_ref[...] = a_ref[(own_ref[1] >> 1) ^ d]


def chain_kernel(own_ref, e_ref, a_ref, b_ref, m_ref, got_ref, *refs, width):
    parts, (x_ref, keep_ref, send_ref) = refs[:-3], refs[-3:]
    core, own = own_ref[0] & 1, own_ref[1]
    total = parts[0][...]
    for part in parts[1:]:
        total = total + part[...]
    x = e_ref[...] - total
    x_ref[...] = x
    block = m_ref.shape[1]
    x_hi, x_lo = split(unfolded(x, width))
    x_both = jnp.concatenate([x_hi, x_lo], axis=1)
    for q in range(a_ref.shape[0]):
        c = own ^ q
        at = pl.ds(pl.multiple_of(c * block, block), block)
        m_hi, m_lo = split(jnp.where(core == 1, got_ref[at, :], m_ref[at, :]))
        both = dot(m_hi, x_both)
        y = both[:, :width] + both[:, width:] + dot(m_lo, x_hi)
        (send_ref if q % 2 else keep_ref)[q // 2] = folded(y) + (a_ref[c] + b_ref[c])


def late_kernel(own_ref, acc_ref, *refs, width):
    out_ref, terms = refs[-1], [refs[i : i + 3] for i in range(0, len(refs) - 1, 3)]
    half = acc_ref.shape[0]

    @pl.when(own_ref[0] >= 2)
    def _():
        out_ref[...] = acc_ref[...]

    @pl.when(own_ref[0] < 2)
    def _():
        rows, block = terms[0][0].shape
        small = block * width // LANES
        sources = [split(jnp.concatenate([unfolded(r[p], width) for p in range(half)], axis=1)) for _, _, r in terms]
        for c in range(rows // block):
            y = None
            at = slice(c * block, (c + 1) * block)
            for (mine_ref, got_ref, _), (x_hi, x_lo) in zip(terms, sources, strict=True):
                m_hi, m_lo = split(jnp.where((own_ref[0] & 1) == 1, got_ref[at], mine_ref[at]))
                term = dot(m_hi, x_hi) + dot(m_hi, x_lo) + dot(m_lo, x_hi)
                y = term if y is None else y + term
            for p in range(half):
                at = (p, slice(c * small, (c + 1) * small))
                out_ref[at] = acc_ref[at] + folded(y[:, p * width : (p + 1) * width])


def fields_kernel(own_ref, e_ref, out_ref, *, slices):
    width = e_ref.shape[2] // slices
    for n in range(e_ref.shape[0]):
        out_ref[n] = folded(flipped(e_ref[n], own_ref[0], slices)[:, :width])


def assemble_kernel(own_ref, parts_ref, *refs, slices):
    out_ref = refs[-1]
    width = out_ref.shape[2] // slices
    order = reversed_bits(slices)
    for n in range(out_ref.shape[0]):
        pieces = [None] * slices
        for i, p in enumerate(order):
            pieces[p] = unfolded(parts_ref[i, n], width)
        out_ref[n] = flipped(jnp.concatenate(pieces, axis=1), own_ref[0], slices)


def assembled(own, every, shape, begin, onto=()):
    owners, count, small, _ = every.shape
    steps, block, cols = shape
    return pl.pallas_call(
        functools.partial(assemble_kernel, slices=owners),
        grid=(1,),
        in_specs=[smem(), pl.BlockSpec(every.shape, lambda i: (0, 0, 0, 0))] + [pl.BlockSpec(memory_space=pl.ANY)] * len(onto),
        out_specs=pl.BlockSpec((count, block, cols), lambda i: (begin // count, 0, 0)),
        out_shape=jax.ShapeDtypeStruct(shape, F32),
        input_output_aliases={2: 0} if onto else {},
        compiler_params=pltpu.CompilerParams(vmem_limit_bytes=24 << 20),
        cost_estimate=LIGHT,
        name="assemble",
    )(own, every, *onto)


def whole_call(kernel, name, out_shapes, *args, scratch=()):
    vmem = pl.BlockSpec(memory_space=pltpu.VMEM)
    out = [jax.ShapeDtypeStruct(s, F32) for s in out_shapes]
    return pl.pallas_call(
        kernel,
        in_specs=[smem()] + [vmem] * (len(args) - 1),
        out_specs=[vmem] * len(out),
        out_shape=out,
        scratch_shapes=[pltpu.VMEM(s, F32) for s in scratch],
        compiler_params=pltpu.CompilerParams(vmem_limit_bytes=40 << 20),
        cost_estimate=LIGHT,
        name=name,
    )(*args)


def sealed(held, *names):
    names = names or tuple(held)
    held.update(zip(names, lax.optimization_barrier(tuple(held[k] for k in names)), strict=True))


def local(lag_matrices, history, excitation):
    owners, columns = lax.axis_size("lag"), lax.axis_size("col")
    owner, column = lax.axis_index("lag"), lax.axis_index("col")
    lags, rows, block = lag_matrices.shape
    steps, _, cols = excitation.shape
    width = cols // owners
    small = block * width // LANES
    bits = bit_count(owners)
    back = steps - 1
    own = jnp.stack([owner, column]).astype(jnp.int32)
    tiles = max(1, rows // 512)
    held = {}

    def stage_pairs(stage):
        def partner(i):
            lag, col = divmod(i, columns)
            if stage < 2:
                return lag * columns + (col ^ 1) if (lag & 1) == stage else (lag ^ 2) * columns + col
            return (lag ^ (1 << stage)) * columns + col

        return [(i, partner(i)) for i in range(owners * columns)]

    def offered(slots):
        return jnp.stack(slots[len(slots) // 2 :])

    def taken(slots, offer, stage):
        got = lax.ppermute(offer, ("lag", "col"), stage_pairs(stage))
        return [slots[i] + got[i] for i in range(len(slots) // 2)]

    def owners_sum(acc):
        for b in range(1, bits):
            half = acc.shape[0] // 2
            got = exchanged(acc[half:], "lag", 1 << b)
            if half == 1:
                return acc[0], got[0]
            acc = acc[:half] + got
        return acc[0], jnp.zeros_like(acc[0])

    def scattered(acc, bit):
        while len(acc) > 4:
            got = exchanged(jnp.stack(acc[1::2]), "col", bit)
            acc = [a + got[i] for i, a in enumerate(acc[0::2])]
            bit *= 2
        return [acc[0]] + [exchanged(acc[d], "col", d * bit) for d in range(1, len(acc))]

    def gathered(x):
        for b in reversed(range(1, bits)):
            x = jnp.concatenate([x, exchanged(x, "lag", 1 << b)], axis=0)
        return x

    def partner_sum(n):
        return held[f"keep{n}"] + exchanged(held[f"send{n}"], "lag", 1)

    def with_tail(n):
        pair = with_carried(own, held["carried"], held[f"keep{n}"], held[f"send{n}"], lag_matrices, n, owners)
        held[f"keep{n}"], held[f"send{n}"] = pair

    newest, tail = staged(own, lag_matrices, history, back)
    top = 1 << (bits - 1)
    held["newest"], held["got"] = newest, lax.ppermute(newest, "lag", [(0, top)])
    held["carried"] = lax.ppermute(tail, "lag", [(i, i + 1) for i in range(owners - 1)])
    partials = bulk(lax.optimization_barrier((own, tail))[0], history, lag_matrices, steps, owners, tiles)
    for n in range(steps):
        held[f"keep{n}"], held[f"send{n}"] = partials[2 * n : 2 * n + 2]
    held["lag2"], held["lag3"] = partials[-2:]
    sealed(held, "send0", "got", "carried")

    got = exchanged(held["send0"], "lag", 1)
    slots = [held["keep0"][i] + got[i] for i in range(owners)]
    held["offer"] = offered(slots)
    sealed(held, "offer", "keep1", "newest")
    slots = taken(slots, held["offer"], 0)
    with_tail(1)
    held["field"] = whole_call(functools.partial(fields_kernel, slices=owners), "fields", [(steps, small, LANES)], own, excitation)[0]
    newest = jnp.where((owner & top) != 0, held["got"], held["newest"])
    for b in reversed(range(1, bits - 1)):
        got = lax.ppermute(newest, "lag", [(i, i + (1 << b)) for i in range(0, owners, 2 << b)])
        newest = jnp.where((owner >> b) & 1 == 1, got, newest)
    held["newest"] = newest
    held["offer"] = offered(slots)
    sealed(held, "offer", "keep1", "send1", "field", "keep2", "newest")
    held["odd"] = lax.ppermute(held["newest"], "lag", [(i, i + 1) for i in range(0, owners, 2)])
    slots = taken(slots, held["offer"], 1)
    for b in range(2, bits):
        slots = taken(slots, offered(slots), b)
    with_tail(2)
    held["past1"] = partner_sum(1)
    held["acc0"] = slots[0]
    sealed(held, "acc0", "keep2", "send2", "past1", "keep3", "odd")
    acc = whole_call(merge_kernel, "merge", [(small, LANES)] * (columns // 2), own, held["acc0"])
    parts = scattered(acc, 2)
    held["mine1"], held["got1"] = owners_sum(held["past1"])
    with_tail(3)
    held["past2"] = partner_sum(2)
    held.update((f"part{i}", part) for i, part in enumerate(parts))
    sealed(held, "keep3", "send3", "past2", "lag2", "mine1", "got1", *(f"part{i}" for i in range(len(parts))))
    a, b = held["mine1"], held["got1"]
    parts = [held[f"part{i}"] for i in range(len(parts))]
    held["past3"] = partner_sum(3)

    shaped = (columns, small, LANES)
    halves = [(columns // 2, small, LANES)] * 2
    shown = []
    for n in range(1, steps):
        x, keep, send = whole_call(
            functools.partial(chain_kernel, width=width), "chain", [(small, LANES), *halves],
            own, held["field"][n - 1], a.reshape(shaped), b.reshape(shaped), held["newest"], held["odd"], *parts,
        )
        shown.append(gathered(x[None]))
        if n + 1 < steps:
            own_lag = lax.optimization_barrier((held[f"lag{n + 1}"], x))[0]
            held[f"odd{n + 1}"] = lax.ppermute(own_lag, "lag", [(0, 1)])
            terms = [v for k in range(2, n + 2) for v in (held[f"lag{k}"], held[f"odd{k}"], shown[n + 1 - k])]
            past = whole_call(
                functools.partial(late_kernel, width=width), "late", [held[f"past{n + 1}"].shape],
                own, held[f"past{n + 1}"], *terms,
            )[0]
            a, b = owners_sum(past)
        acc = keep + exchanged(send, "col", 1)
        parts = scattered([acc[i] for i in range(columns // 2)], 2)
    early = jnp.stack(shown, axis=1)
    early = jnp.concatenate([early, exchanged(early, "lag", 1)], axis=0)
    held["dens"] = assembled(own, early, excitation.shape, 0)
    held.update((f"part{i}", part) for i, part in enumerate(parts))
    sealed(held, "dens", *(f"part{i}" for i in range(len(parts))))
    x = held["field"][steps - 1] - functools.reduce(jnp.add, [held[f"part{i}"] for i in range(len(parts))])
    newest = gathered(x[None])
    newest = jnp.concatenate([newest, exchanged(newest, "lag", 1)], axis=0)
    return assembled(own, newest[:, None], excitation.shape, steps - 1, [held["dens"]])


def solution(mesh):
    return jax.shard_map(
        local,
        mesh=mesh,
        in_specs=(P("lag", None, "col"), P("lag", "col", None), P(None, "col", None)),
        out_specs=P(None, "col", None),
        check_vma=False,
    )
```

```python
import functools

import jax
import jax.numpy as jnp
from jax import lax
from jax.experimental import pallas as pl
from jax.experimental.pallas import tpu as pltpu
from jax.sharding import PartitionSpec as P

LANES = 128
BF = jnp.bfloat16
F32 = jnp.float32
LIGHT = pl.CostEstimate(flops=1, bytes_accessed=1, transcendentals=0)
KINDS = tuple((outer, inner) for outer in (1, 2, 3) for inner in (1, 2, 3))
MEMBERS = {1: (1,), 2: (0, 1), 3: (0,)}


def swap_pairs(axis, bit):
    return [(i, i ^ bit) for i in range(lax.axis_size(axis))]


def exchanged(value, axis, bit):
    return lax.ppermute(value, axis, swap_pairs(axis, bit))


def bit_count(n):
    return n.bit_length() - 1


def reversed_bits(n):
    bits = bit_count(n)
    return [sum(((i >> b) & 1) << (bits - 1 - b) for b in range(bits)) for i in range(n)]


def split(v):
    hi = v.astype(BF)
    return hi, (v - hi.astype(F32)).astype(BF)


def dot(a, b):
    return jnp.dot(a, b, preferred_element_type=F32)


def flipped(v, own, slices):
    cols = v.shape[-1]
    width = cols // slices
    for b in range(bit_count(slices)):
        step = width << b
        swapped = jnp.concatenate(
            [v[:, (start ^ step) : (start ^ step) + step] for start in range(0, cols, step)], axis=1
        )
        v = jnp.where(((own >> b) & 1) == 1, swapped, v)
    return v


def folded(v):
    rows, width = v.shape
    parts = LANES // width
    step = rows // parts
    return jnp.concatenate([v[s * step : (s + 1) * step] for s in range(parts)], axis=1) if parts > 1 else v


def unfolded(v, width):
    parts = LANES // width
    return jnp.concatenate([v[:, s * width : (s + 1) * width] for s in range(parts)], axis=0) if parts > 1 else v


def source_sums(get, outer, inner, base):
    def along(inner_offset):
        if outer == 1:
            return get(base + 2 + inner_offset) - get(base + inner_offset)
        if outer == 2:
            return get(base + inner_offset)
        return get(base + inner_offset) - get(base - 2 + inner_offset)

    if inner == 1:
        return along(1) - along(0)
    if inner == 2:
        return along(0)
    return along(0) - along(-1)


def prepare_sources(kinds, get, own, slices, groups, hi_ref, lo_ref):
    block = hi_ref.shape[1] // groups
    for i, (outer, inner) in enumerate(kinds):
        for g in range(groups):
            hi, lo = split(flipped(source_sums(get, outer, inner, 4 * g), own, slices))
            hi_ref[i, g * block : (g + 1) * block, :] = hi
            lo_ref[i, g * block : (g + 1) * block, :] = lo


def write_folded(y, block, keep_ref, send_ref, slices):
    width = y.shape[1] // slices
    small = block * width // LANES
    half = slices // 2
    for b in range(y.shape[0] // block):
        rows = y[b * block : (b + 1) * block]
        for i, p in enumerate(reversed_bits(slices)):
            piece = folded(rows[:, p * width : (p + 1) * width])
            (send_ref if i // half else keep_ref)[i % half, b * small : (b + 1) * small, :] = piece


def slot(core, x_part, y_part, half):
    top, low = y_part // (half // 2), y_part % (half // 2)
    return jnp.where(core == 0, (x_part * 2 + top) * (half // 2) + low, (top * 2 + x_part) * (half // 2) + low)


def write_slots(y, block, own_ref, keep_ref, send_ref, slices):
    width = y.shape[1] // slices
    half = slices // 2
    core, side = own_ref[0] & 1, own_ref[1] & 1
    for b in range(y.shape[0] // block):
        rows = y[b * block : (b + 1) * block]
        for i, p in enumerate(reversed_bits(slices)):
            piece = folded(rows[:, p * width : (p + 1) * width])
            at = slot(core ^ (i // half), (b & 1) ^ side, i % half, half)
            (send_ref if i // half else keep_ref)[at, b // 2, :, :] = piece


def products(kinds, a_ref, hi_ref, lo_ref):
    groups = a_ref.shape[0]
    out = []
    for i, (outer, inner) in enumerate(kinds):
        his, los = [], []
        for g in range(groups):
            total = None
            for u in MEMBERS[outer]:
                for v in MEMBERS[inner]:
                    term = a_ref[g, u, v]
                    total = term if total is None else total + term
            hi, lo = split(total)
            his.append(hi)
            los.append(lo)
        hi, lo = jnp.concatenate(his, axis=1), jnp.concatenate(los, axis=1)
        out.append(dot(hi, hi_ref[i]) + dot(hi, lo_ref[i]) + dot(lo, hi_ref[i]))
    return out


def bulk_kernel(own_ref, history_ref, a_ref, *refs, slices, block):
    outs, (second_ref, third_ref, hi_ref, lo_ref, tiles_ref, sems) = refs[:-6], refs[-6:]
    step, steps = pl.program_id(0), pl.num_programs(0)
    tile = tiles_ref.shape[4]

    def fetch(i):
        rows = pl.ds(pl.multiple_of(i * tile, tile), tile)
        return pltpu.make_async_copy(a_ref.at[:, :, :, rows, :], tiles_ref.at[i % 2], sems.at[i % 2])

    @pl.when(step == 0)
    def _():
        fetch(0).start()

    @pl.when(step + 1 < steps)
    def _():
        fetch(step + 1).start()

    @pl.when(step == 0)
    def _():
        def get(i):
            return history_ref[i] if i >= 0 else jnp.zeros(history_ref.shape[1:], F32)

        prepare_sources(KINDS, get, own_ref[0], slices, a_ref.shape[0], hi_ref, lo_ref)

    fetch(step).wait()
    a_ref = tiles_ref.at[step % 2]
    second_ref[...] = a_ref[0, 0, 1]
    third_ref[...] = a_ref[0, 1, 0]
    p11, p12, p13, p21, p22, p23, p31, p32, p33 = products(KINDS, a_ref, hi_ref, lo_ref)
    write_slots((p12 + p22) + (p11 + p21), block, own_ref, outs[0], outs[1], slices)
    times = ((p12 + p22) - (p13 + p23), (p21 + p22) - (p31 + p32), (p22 - p23) - (p32 - p33))
    for n, y in enumerate(times):
        write_folded(y, block, outs[2 * n + 2], outs[2 * n + 3], slices)


def carried_kernel(own_ref, tail_ref, keep_in, send_in, *refs, slices):
    matrices, (keep_ref, send_ref) = refs[:-2], refs[-2:]
    back, block = tail_ref.shape[:2]
    count = len(matrices)
    width = tail_ref.shape[2] // slices
    small = block * width // LANES
    half = slices // 2
    x = jnp.concatenate([flipped(tail_ref[back - count + j], own_ref[0], slices) for j in range(count)], axis=0)
    x_hi, x_lo = split(x)
    for c in range(matrices[0].shape[1] // block):
        m_hi, m_lo = split(jnp.concatenate([r[0, c * block : (c + 1) * block, :] for r in matrices], axis=1))
        y = dot(m_hi, x_hi) + dot(m_hi, x_lo) + dot(m_lo, x_hi)
        for i, p in enumerate(reversed_bits(slices)):
            at = (i % half, slice(c * small, (c + 1) * small))
            from_ref, to_ref = (send_in, send_ref) if i // half else (keep_in, keep_ref)
            to_ref[at] = from_ref[at] + folded(y[:, p * width : (p + 1) * width])


def with_carried(own, tail, keep, send, matrices, count, slices):
    lags, rows, block = matrices.shape
    return pl.pallas_call(
        functools.partial(carried_kernel, slices=slices),
        grid=(1,),
        in_specs=[smem()]
        + [pl.BlockSpec(v.shape, lambda i: (0, 0, 0)) for v in (tail, keep, send)]
        + [pl.BlockSpec((1, rows, block), lambda i, j=j: (j, 0, 0)) for j in range(count)],
        out_specs=[pl.BlockSpec(keep.shape, lambda i: (0, 0, 0))] * 2,
        out_shape=[jax.ShapeDtypeStruct(keep.shape, F32)] * 2,
        compiler_params=pltpu.CompilerParams(vmem_limit_bytes=40 << 20),
        cost_estimate=LIGHT,
        name="carried",
    )(own, tail, keep, send, *[matrices] * count)


def smem():
    return pl.BlockSpec(memory_space=pltpu.SMEM)


def bulk(own, history, matrices, steps, slices, tiles):
    lags, rows, block = matrices.shape
    cols = history.shape[2]
    groups = lags // 4
    tile = rows // tiles
    small = block * (cols // slices) // LANES
    pairs = rows // block // 2
    flat = jax.ShapeDtypeStruct((slices // 2, 2 * pairs * small, LANES), F32)
    flat_spec = pl.BlockSpec((slices // 2, 2 * pairs * small // tiles, LANES), lambda i: (0, i, 0))
    slots = jax.ShapeDtypeStruct((slices, pairs, small, LANES), F32)
    slots_spec = pl.BlockSpec((slices, pairs // tiles, small, LANES), lambda i: (0, i, 0, 0))
    return pl.pallas_call(
        functools.partial(bulk_kernel, slices=slices, block=block),
        grid=(tiles,),
        in_specs=[
            smem(),
            pl.BlockSpec(history.shape, lambda i: (0, 0, 0)),
            pl.BlockSpec(memory_space=pl.ANY),
        ],
        out_specs=[slots_spec] * 2 + [flat_spec] * (2 * steps - 2) + [pl.BlockSpec((tile, block), lambda i: (i, 0))] * 2,
        out_shape=[slots] * 2 + [flat] * (2 * steps - 2) + [jax.ShapeDtypeStruct((rows, block), F32)] * 2,
        scratch_shapes=[
            *[pltpu.VMEM((len(KINDS), groups * block, cols), BF)] * 2,
            pltpu.VMEM((2, groups, 2, 2, tile, block), F32),
            pltpu.SemaphoreType.DMA((2,)),
        ],
        compiler_params=pltpu.CompilerParams(vmem_limit_bytes=61 << 20),
        cost_estimate=pl.CostEstimate(
            flops=2 * 4 * len(KINDS) * groups * rows * block * cols,
            bytes_accessed=4 * matrices.size,
            transcendentals=0,
        ),
        name="bulk",
    )(own, history, matrices.reshape(groups, 2, 2, rows, block))


def stage_kernel(own_ref, a_ref, *refs):
    slabs, (newest_ref, tail_ref) = refs[:-2], refs[-2:]
    newest_ref[...] = a_ref[0]
    for i, slab in enumerate(slabs):
        tail_ref[i] = slab[0]


def staged(own, matrices, history, back):
    lags, rows, block = matrices.shape
    cols = history.shape[2]
    shapes = [(rows, block), (back, block, cols)]
    return pl.pallas_call(
        stage_kernel,
        grid=(1,),
        in_specs=[smem(), pl.BlockSpec((1, rows, block), lambda i: (0, 0, 0))]
        + [pl.BlockSpec((1, block, cols), lambda i, at=lags - back + k: (at, 0, 0)) for k in range(back)],
        out_specs=[pl.BlockSpec(s, lambda i, r=len(s): (0,) * r) for s in shapes],
        out_shape=[jax.ShapeDtypeStruct(s, F32) for s in shapes],
        compiler_params=pltpu.CompilerParams(vmem_limit_bytes=61 << 20),
        cost_estimate=LIGHT,
        name="stage",
    )(own, matrices, *[history] * back)


def merge_kernel(own_ref, a_ref, *out_refs):
    for d, out_ref in enumerate(out_refs):
        out_ref[...] = a_ref[(own_ref[1] >> 1) ^ d]


def chain_kernel(own_ref, e_ref, a_ref, b_ref, m_ref, got_ref, *refs, width):
    parts, (x_ref, keep_ref, send_ref) = refs[:-3], refs[-3:]
    core, own = own_ref[0] & 1, own_ref[1]
    total = parts[0][...]
    for part in parts[1:]:
        total = total + part[...]
    x = e_ref[...] - total
    x_ref[...] = x
    block = m_ref.shape[1]
    x_hi, x_lo = split(unfolded(x, width))
    x_both = jnp.concatenate([x_hi, x_lo], axis=1)
    for q in range(a_ref.shape[0]):
        c = own ^ q
        at = pl.ds(pl.multiple_of(c * block, block), block)
        m_hi, m_lo = split(jnp.where(core == 1, got_ref[at, :], m_ref[at, :]))
        both = dot(m_hi, x_both)
        y = both[:, :width] + both[:, width:] + dot(m_lo, x_hi)
        (send_ref if q % 2 else keep_ref)[q // 2] = folded(y) + (a_ref[c] + b_ref[c])


def late_kernel(own_ref, acc_ref, *refs, width):
    out_ref, terms = refs[-1], [refs[i : i + 3] for i in range(0, len(refs) - 1, 3)]
    half = acc_ref.shape[0]

    @pl.when(own_ref[0] >= 2)
    def _():
        out_ref[...] = acc_ref[...]

    @pl.when(own_ref[0] < 2)
    def _():
        rows, block = terms[0][0].shape
        small = block * width // LANES
        sources = [split(jnp.concatenate([unfolded(r[p], width) for p in range(half)], axis=1)) for _, _, r in terms]
        for c in range(rows // block):
            y = None
            at = slice(c * block, (c + 1) * block)
            for (mine_ref, got_ref, _), (x_hi, x_lo) in zip(terms, sources, strict=True):
                m_hi, m_lo = split(jnp.where((own_ref[0] & 1) == 1, got_ref[at], mine_ref[at]))
                term = dot(m_hi, x_hi) + dot(m_hi, x_lo) + dot(m_lo, x_hi)
                y = term if y is None else y + term
            for p in range(half):
                at = (p, slice(c * small, (c + 1) * small))
                out_ref[at] = acc_ref[at] + folded(y[:, p * width : (p + 1) * width])


def fields_kernel(own_ref, e_ref, out_ref, *, slices):
    width = e_ref.shape[2] // slices
    for n in range(e_ref.shape[0]):
        out_ref[n] = folded(flipped(e_ref[n], own_ref[0], slices)[:, :width])


def assemble_kernel(own_ref, parts_ref, *refs, slices):
    out_ref = refs[-1]
    width = out_ref.shape[2] // slices
    order = reversed_bits(slices)
    for n in range(out_ref.shape[0]):
        pieces = [None] * slices
        for i, p in enumerate(order):
            pieces[p] = unfolded(parts_ref[i, n], width)
        out_ref[n] = flipped(jnp.concatenate(pieces, axis=1), own_ref[0], slices)


def assembled(own, every, shape, begin, onto=()):
    owners, count, small, _ = every.shape
    steps, block, cols = shape
    return pl.pallas_call(
        functools.partial(assemble_kernel, slices=owners),
        grid=(1,),
        in_specs=[smem(), pl.BlockSpec(every.shape, lambda i: (0, 0, 0, 0))] + [pl.BlockSpec(memory_space=pl.ANY)] * len(onto),
        out_specs=pl.BlockSpec((count, block, cols), lambda i: (begin // count, 0, 0)),
        out_shape=jax.ShapeDtypeStruct(shape, F32),
        input_output_aliases={2: 0} if onto else {},
        compiler_params=pltpu.CompilerParams(vmem_limit_bytes=24 << 20),
        cost_estimate=LIGHT,
        name="assemble",
    )(own, every, *onto)


def whole_call(kernel, name, out_shapes, *args, scratch=()):
    vmem = pl.BlockSpec(memory_space=pltpu.VMEM)
    out = [jax.ShapeDtypeStruct(s, F32) for s in out_shapes]
    return pl.pallas_call(
        kernel,
        in_specs=[smem()] + [vmem] * (len(args) - 1),
        out_specs=[vmem] * len(out),
        out_shape=out,
        scratch_shapes=[pltpu.VMEM(s, F32) for s in scratch],
        compiler_params=pltpu.CompilerParams(vmem_limit_bytes=40 << 20),
        cost_estimate=LIGHT,
        name=name,
    )(*args)


def sealed(held, *names):
    names = names or tuple(held)
    held.update(zip(names, lax.optimization_barrier(tuple(held[k] for k in names)), strict=True))


def local(lag_matrices, history, excitation):
    owners, columns = lax.axis_size("lag"), lax.axis_size("col")
    owner, column = lax.axis_index("lag"), lax.axis_index("col")
    lags, rows, block = lag_matrices.shape
    steps, _, cols = excitation.shape
    width = cols // owners
    small = block * width // LANES
    bits = bit_count(owners)
    back = steps - 1
    own = jnp.stack([owner, column]).astype(jnp.int32)
    tiles = max(1, rows // 512)
    held = {}

    def stage_pairs(stage):
        def partner(i):
            lag, col = divmod(i, columns)
            if stage < 2:
                return lag * columns + (col ^ 1) if (lag & 1) == stage else (lag ^ 2) * columns + col
            return (lag ^ (1 << stage)) * columns + col

        return [(i, partner(i)) for i in range(owners * columns)]

    def offered(slots):
        return jnp.stack(slots[len(slots) // 2 :])

    def taken(slots, offer, stage):
        got = lax.ppermute(offer, ("lag", "col"), stage_pairs(stage))
        return [slots[i] + got[i] for i in range(len(slots) // 2)]

    def owners_sum(acc):
        for b in range(1, bits):
            half = acc.shape[0] // 2
            got = exchanged(acc[half:], "lag", 1 << b)
            if half == 1:
                return acc[0], got[0]
            acc = acc[:half] + got
        return acc[0], jnp.zeros_like(acc[0])

    def scattered(acc, bit):
        while len(acc) > 4:
            got = exchanged(jnp.stack(acc[1::2]), "col", bit)
            acc = [a + got[i] for i, a in enumerate(acc[0::2])]
            bit *= 2
        return [acc[0]] + [exchanged(acc[d], "col", d * bit) for d in range(1, len(acc))]

    def gathered(x):
        for b in reversed(range(1, bits)):
            x = jnp.concatenate([x, exchanged(x, "lag", 1 << b)], axis=0)
        return x

    def partner_sum(n):
        return held[f"keep{n}"] + exchanged(held[f"send{n}"], "lag", 1)

    def with_tail(n):
        pair = with_carried(own, held["carried"], held[f"keep{n}"], held[f"send{n}"], lag_matrices, n, owners)
        held[f"keep{n}"], held[f"send{n}"] = pair

    newest, tail = staged(own, lag_matrices, history, back)
    top = 1 << (bits - 1)
    held["newest"], held["got"] = newest, lax.ppermute(newest, "lag", [(0, top)])
    held["carried"] = lax.ppermute(tail, "lag", [(i, i + 1) for i in range(owners - 1)])
    partials = bulk(own, history, lag_matrices, steps, owners, tiles)
    for n in range(steps):
        held[f"keep{n}"], held[f"send{n}"] = partials[2 * n : 2 * n + 2]
    held["lag2"], held["lag3"] = partials[-2:]
    sealed(held, "send0", "got", "carried")

    got = exchanged(held["send0"], "lag", 1)
    slots = [held["keep0"][i] + got[i] for i in range(owners)]
    held["offer"] = offered(slots)
    sealed(held, "offer", "keep1", "newest")
    slots = taken(slots, held["offer"], 0)
    with_tail(1)
    held["field"] = whole_call(functools.partial(fields_kernel, slices=owners), "fields", [(steps, small, LANES)], own, excitation)[0]
    newest = jnp.where((owner & top) != 0, held["got"], held["newest"])
    for b in reversed(range(1, bits - 1)):
        got = lax.ppermute(newest, "lag", [(i, i + (1 << b)) for i in range(0, owners, 2 << b)])
        newest = jnp.where((owner >> b) & 1 == 1, got, newest)
    held["newest"] = newest
    held["offer"] = offered(slots)
    sealed(held, "offer", "keep1", "send1", "field", "keep2", "newest")
    held["odd"] = lax.ppermute(held["newest"], "lag", [(i, i + 1) for i in range(0, owners, 2)])
    slots = taken(slots, held["offer"], 1)
    for b in range(2, bits):
        slots = taken(slots, offered(slots), b)
    with_tail(2)
    held["past1"] = partner_sum(1)
    held["acc0"] = slots[0]
    sealed(held, "acc0", "keep2", "send2", "keep3", "odd")
    acc = whole_call(merge_kernel, "merge", [(small, LANES)] * (columns // 2), own, held["acc0"])
    parts = scattered(acc, 2)
    held["mine1"], held["got1"] = owners_sum(held["past1"])
    with_tail(3)
    held["past2"] = partner_sum(2)
    held.update((f"part{i}", part) for i, part in enumerate(parts))
    sealed(held, "keep3", "send3", "past2", "lag2", "mine1", "got1", *(f"part{i}" for i in range(len(parts))))
    a, b = held["mine1"], held["got1"]
    parts = [held[f"part{i}"] for i in range(len(parts))]

    shaped = (columns, small, LANES)
    halves = [(columns // 2, small, LANES)] * 2
    shown = []
    for n in range(1, steps):
        x, keep, send = whole_call(
            functools.partial(chain_kernel, width=width), "chain", [(small, LANES), *halves],
            own, held["field"][n - 1], a.reshape(shaped), b.reshape(shaped), held["newest"], held["odd"], *parts,
        )
        if n + 1 < steps:
            if n == 1:
                held["x"] = x
                sealed(held, "x", "lag2", "send3")
                x = held["x"]
                held["past3"] = partner_sum(3)
            else:
                held["x"] = x
                sealed(held, "x", "lag3", "past3")
                x = held["x"]
            held[f"odd{n + 1}"] = lax.ppermute(held[f"lag{n + 1}"], "lag", [(0, 1)])
            shown.append(gathered(x[None]))
            terms = [v for k in range(2, n + 2) for v in (held[f"lag{k}"], held[f"odd{k}"], shown[n + 1 - k])]
            past = whole_call(
                functools.partial(late_kernel, width=width), "late", [held[f"past{n + 1}"].shape],
                own, held[f"past{n + 1}"], *terms,
            )[0]
            a, b = owners_sum(past)
        else:
            shown.append(gathered(x[None]))
        acc = keep + exchanged(send, "col", 1)
        parts = scattered([acc[i] for i in range(columns // 2)], 2)
    early = jnp.stack(shown, axis=1)
    early = jnp.concatenate([early, exchanged(early, "lag", 1)], axis=0)
    held["dens"] = assembled(own, early, excitation.shape, 0)
    held.update((f"part{i}", part) for i, part in enumerate(parts))
    sealed(held, "dens", *(f"part{i}" for i in range(len(parts))))
    x = held["field"][steps - 1] - functools.reduce(jnp.add, [held[f"part{i}"] for i in range(len(parts))])
    newest = gathered(x[None])
    newest = jnp.concatenate([newest, exchanged(newest, "lag", 1)], axis=0)
    return assembled(own, newest[:, None], excitation.shape, steps - 1, [held["dens"]])


def solution(mesh):
    return jax.shard_map(
        local,
        mesh=mesh,
        in_specs=(P("lag", None, "col"), P("lag", "col", None), P(None, "col", None)),
        out_specs=P(None, "col", None),
        check_vma=False,
    )
```

```python
import functools

import jax
import jax.numpy as jnp
from jax import lax
from jax.experimental import pallas as pl
from jax.experimental.pallas import tpu as pltpu
from jax.sharding import PartitionSpec as P

LANES = 128
BF = jnp.bfloat16
F32 = jnp.float32
PLACE = 16
LIGHT = pl.CostEstimate(flops=1, bytes_accessed=1, transcendentals=0)
KINDS = tuple((outer, inner) for outer in (1, 2, 3) for inner in (1, 2, 3))
MEMBERS = {1: (1,), 2: (0, 1), 3: (0,)}


def swap_pairs(axis, bit):
    return [(i, i ^ bit) for i in range(lax.axis_size(axis))]


def exchanged(value, axis, bit):
    return lax.ppermute(value, axis, swap_pairs(axis, bit))


def bit_count(n):
    return n.bit_length() - 1


def reversed_bits(n):
    bits = bit_count(n)
    return [sum(((i >> b) & 1) << (bits - 1 - b) for b in range(bits)) for i in range(n)]


def owner_of(own_ref):
    return own_ref[0] & ((1 << PLACE) - 1)


def column_of(own_ref):
    return own_ref[0] >> PLACE


def split(v):
    hi = v.astype(BF)
    return hi, (v - hi.astype(F32)).astype(BF)


def dot(a, b):
    return jnp.dot(a, b, preferred_element_type=F32)


def flipped(v, own, slices):
    cols = v.shape[-1]
    width = cols // slices
    for b in range(bit_count(slices)):
        step = width << b
        swapped = jnp.concatenate(
            [v[:, (start ^ step) : (start ^ step) + step] for start in range(0, cols, step)], axis=1
        )
        v = jnp.where(((own >> b) & 1) == 1, swapped, v)
    return v


def folded(v):
    rows, width = v.shape
    parts = LANES // width
    step = rows // parts
    return jnp.concatenate([v[s * step : (s + 1) * step] for s in range(parts)], axis=1) if parts > 1 else v


def unfolded(v, width):
    parts = LANES // width
    return jnp.concatenate([v[:, s * width : (s + 1) * width] for s in range(parts)], axis=0) if parts > 1 else v


def source_sums(get, outer, inner, base):
    def along(inner_offset):
        if outer == 1:
            return get(base + 2 + inner_offset) - get(base + inner_offset)
        if outer == 2:
            return get(base + inner_offset)
        return get(base + inner_offset) - get(base - 2 + inner_offset)

    if inner == 1:
        return along(1) - along(0)
    if inner == 2:
        return along(0)
    return along(0) - along(-1)


def prepare_sources(kinds, get, own, slices, groups, hi_ref, lo_ref):
    block = hi_ref.shape[1] // groups
    for i, (outer, inner) in enumerate(kinds):
        for g in range(groups):
            hi, lo = split(flipped(source_sums(get, outer, inner, 4 * g), own, slices))
            hi_ref[i, g * block : (g + 1) * block, :] = hi
            lo_ref[i, g * block : (g + 1) * block, :] = lo


def write_folded(y, block, keep_ref, send_ref, slices):
    width = y.shape[1] // slices
    small = block * width // LANES
    half = slices // 2
    for b in range(y.shape[0] // block):
        rows = y[b * block : (b + 1) * block]
        for i, p in enumerate(reversed_bits(slices)):
            piece = folded(rows[:, p * width : (p + 1) * width])
            (send_ref if i // half else keep_ref)[i % half, b * small : (b + 1) * small, :] = piece


def slot(core, x_part, y_part, half):
    top, low = y_part // (half // 2), y_part % (half // 2)
    return jnp.where(core == 0, (x_part * 2 + top) * (half // 2) + low, (top * 2 + x_part) * (half // 2) + low)


def write_slots(y, block, own_ref, keep_ref, send_ref, slices):
    width = y.shape[1] // slices
    half = slices // 2
    core, side = owner_of(own_ref) & 1, column_of(own_ref) & 1
    for b in range(y.shape[0] // block):
        rows = y[b * block : (b + 1) * block]
        for i, p in enumerate(reversed_bits(slices)):
            piece = folded(rows[:, p * width : (p + 1) * width])
            at = slot(core ^ (i // half), (b & 1) ^ side, i % half, half)
            (send_ref if i // half else keep_ref)[at, b // 2, :, :] = piece


def products(kinds, a_ref, hi_ref, lo_ref):
    groups = a_ref.shape[0]
    out = []
    for i, (outer, inner) in enumerate(kinds):
        his, los = [], []
        for g in range(groups):
            total = None
            for u in MEMBERS[outer]:
                for v in MEMBERS[inner]:
                    term = a_ref[g, u, v]
                    total = term if total is None else total + term
            hi, lo = split(total)
            his.append(hi)
            los.append(lo)
        hi, lo = jnp.concatenate(his, axis=1), jnp.concatenate(los, axis=1)
        out.append(dot(hi, hi_ref[i]) + dot(hi, lo_ref[i]) + dot(lo, hi_ref[i]))
    return out


def bulk_kernel(own_ref, history_ref, a_ref, *refs, slices, block):
    outs, (second_ref, third_ref, hi_ref, lo_ref, tiles_ref, sems) = refs[:-6], refs[-6:]
    step, steps = pl.program_id(0), pl.num_programs(0)
    tile = tiles_ref.shape[4]

    def fetch(i):
        rows = pl.ds(pl.multiple_of(i * tile, tile), tile)
        return pltpu.make_async_copy(a_ref.at[:, :, :, rows, :], tiles_ref.at[i % 2], sems.at[i % 2])

    @pl.when(step == 0)
    def _():
        fetch(0).start()

    @pl.when(step + 1 < steps)
    def _():
        fetch(step + 1).start()

    @pl.when(step == 0)
    def _():
        def get(i):
            return history_ref[i] if i >= 0 else jnp.zeros(history_ref.shape[1:], F32)

        prepare_sources(KINDS, get, owner_of(own_ref), slices, a_ref.shape[0], hi_ref, lo_ref)

    fetch(step).wait()
    a_ref = tiles_ref.at[step % 2]
    second_ref[...] = a_ref[0, 0, 1]
    third_ref[...] = a_ref[0, 1, 0]
    p11, p12, p13, p21, p22, p23, p31, p32, p33 = products(KINDS, a_ref, hi_ref, lo_ref)
    write_slots((p12 + p22) + (p11 + p21), block, own_ref, outs[0], outs[1], slices)
    times = ((p12 + p22) - (p13 + p23), (p21 + p22) - (p31 + p32), (p22 - p23) - (p32 - p33))
    for n, y in enumerate(times):
        write_folded(y, block, outs[2 * n + 2], outs[2 * n + 3], slices)


def carried_kernel(own_ref, tail_ref, keep_in, send_in, *refs, slices):
    matrices, (keep_ref, send_ref) = refs[:-2], refs[-2:]
    back, block = tail_ref.shape[:2]
    count = len(matrices)
    width = tail_ref.shape[2] // slices
    small = block * width // LANES
    half = slices // 2
    x = jnp.concatenate([flipped(tail_ref[back - count + j], owner_of(own_ref), slices) for j in range(count)], axis=0)
    x_hi, x_lo = split(x)
    for c in range(matrices[0].shape[1] // block):
        m_hi, m_lo = split(jnp.concatenate([r[0, c * block : (c + 1) * block, :] for r in matrices], axis=1))
        y = dot(m_hi, x_hi) + dot(m_hi, x_lo) + dot(m_lo, x_hi)
        for i, p in enumerate(reversed_bits(slices)):
            at = (i % half, slice(c * small, (c + 1) * small))
            from_ref, to_ref = (send_in, send_ref) if i // half else (keep_in, keep_ref)
            to_ref[at] = from_ref[at] + folded(y[:, p * width : (p + 1) * width])


def with_carried(own, tail, keep, send, matrices, count, slices):
    lags, rows, block = matrices.shape
    return pl.pallas_call(
        functools.partial(carried_kernel, slices=slices),
        grid=(1,),
        in_specs=[smem()]
        + [pl.BlockSpec(v.shape, lambda i: (0, 0, 0)) for v in (tail, keep, send)]
        + [pl.BlockSpec((1, rows, block), lambda i, j=j: (j, 0, 0)) for j in range(count)],
        out_specs=[pl.BlockSpec(keep.shape, lambda i: (0, 0, 0))] * 2,
        out_shape=[jax.ShapeDtypeStruct(keep.shape, F32)] * 2,
        compiler_params=pltpu.CompilerParams(vmem_limit_bytes=40 << 20),
        cost_estimate=LIGHT,
        name="carried",
    )(own, tail, keep, send, *[matrices] * count)


def smem():
    return pl.BlockSpec(memory_space=pltpu.SMEM)


def bulk(own, history, matrices, steps, slices, tiles):
    lags, rows, block = matrices.shape
    cols = history.shape[2]
    groups = lags // 4
    tile = rows // tiles
    small = block * (cols // slices) // LANES
    pairs = rows // block // 2
    flat = jax.ShapeDtypeStruct((slices // 2, 2 * pairs * small, LANES), F32)
    flat_spec = pl.BlockSpec((slices // 2, 2 * pairs * small // tiles, LANES), lambda i: (0, i, 0))
    slots = jax.ShapeDtypeStruct((slices, pairs, small, LANES), F32)
    slots_spec = pl.BlockSpec((slices, pairs // tiles, small, LANES), lambda i: (0, i, 0, 0))
    return pl.pallas_call(
        functools.partial(bulk_kernel, slices=slices, block=block),
        grid=(tiles,),
        in_specs=[
            smem(),
            pl.BlockSpec(history.shape, lambda i: (0, 0, 0)),
            pl.BlockSpec(memory_space=pl.ANY),
        ],
        out_specs=[slots_spec] * 2 + [flat_spec] * (2 * steps - 2) + [pl.BlockSpec((tile, block), lambda i: (i, 0))] * 2,
        out_shape=[slots] * 2 + [flat] * (2 * steps - 2) + [jax.ShapeDtypeStruct((rows, block), F32)] * 2,
        scratch_shapes=[
            *[pltpu.VMEM((len(KINDS), groups * block, cols), BF)] * 2,
            pltpu.VMEM((2, groups, 2, 2, tile, block), F32),
            pltpu.SemaphoreType.DMA((2,)),
        ],
        compiler_params=pltpu.CompilerParams(vmem_limit_bytes=61 << 20),
        cost_estimate=pl.CostEstimate(
            flops=2 * 4 * len(KINDS) * groups * rows * block * cols,
            bytes_accessed=4 * matrices.size,
            transcendentals=0,
        ),
        name="bulk",
    )(own, history, matrices.reshape(groups, 2, 2, rows, block))


def stage_kernel(own_ref, a_ref, *refs):
    slabs, (newest_ref, tail_ref) = refs[:-2], refs[-2:]
    newest_ref[...] = a_ref[0]
    for i, slab in enumerate(slabs):
        tail_ref[i] = slab[0]


def staged(own, matrices, history, back):
    lags, rows, block = matrices.shape
    cols = history.shape[2]
    shapes = [(rows, block), (back, block, cols)]
    return pl.pallas_call(
        stage_kernel,
        grid=(1,),
        in_specs=[smem(), pl.BlockSpec((1, rows, block), lambda i: (0, 0, 0))]
        + [pl.BlockSpec((1, block, cols), lambda i, at=lags - back + k: (at, 0, 0)) for k in range(back)],
        out_specs=[pl.BlockSpec(s, lambda i, r=len(s): (0,) * r) for s in shapes],
        out_shape=[jax.ShapeDtypeStruct(s, F32) for s in shapes],
        compiler_params=pltpu.CompilerParams(vmem_limit_bytes=61 << 20),
        cost_estimate=LIGHT,
        name="stage",
    )(own, matrices, *[history] * back)


def merge_kernel(own_ref, a_ref, *out_refs):
    for d, out_ref in enumerate(out_refs):
        out_ref[...] = a_ref[(column_of(own_ref) >> 1) ^ d]


def chain_kernel(own_ref, e_ref, a_ref, b_ref, m_ref, got_ref, *refs, width):
    parts, (x_ref, keep_ref, send_ref) = refs[:-3], refs[-3:]
    core, own = owner_of(own_ref) & 1, column_of(own_ref)
    total = parts[0][...]
    for part in parts[1:]:
        total = total + part[...]
    x = e_ref[...] - total
    x_ref[...] = x
    block = m_ref.shape[1]
    x_hi, x_lo = split(unfolded(x, width))
    x_both = jnp.concatenate([x_hi, x_lo], axis=1)
    for q in range(a_ref.shape[0]):
        c = own ^ q
        at = pl.ds(pl.multiple_of(c * block, block), block)
        m_hi, m_lo = split(jnp.where(core == 1, got_ref[at, :], m_ref[at, :]))
        both = dot(m_hi, x_both)
        y = both[:, :width] + both[:, width:] + dot(m_lo, x_hi)
        (send_ref if q % 2 else keep_ref)[q // 2] = folded(y) + (a_ref[c] + b_ref[c])


def late_kernel(own_ref, acc_ref, *refs, width):
    out_ref, terms = refs[-1], [refs[i : i + 3] for i in range(0, len(refs) - 1, 3)]
    half = acc_ref.shape[0]

    @pl.when(owner_of(own_ref) >= 2)
    def _():
        out_ref[...] = acc_ref[...]

    @pl.when(owner_of(own_ref) < 2)
    def _():
        rows, block = terms[0][0].shape
        small = block * width // LANES
        sources = [split(jnp.concatenate([unfolded(r[p], width) for p in range(half)], axis=1)) for _, _, r in terms]
        for c in range(rows // block):
            y = None
            at = slice(c * block, (c + 1) * block)
            for (mine_ref, got_ref, _), (x_hi, x_lo) in zip(terms, sources, strict=True):
                m_hi, m_lo = split(jnp.where((owner_of(own_ref) & 1) == 1, got_ref[at], mine_ref[at]))
                term = dot(m_hi, x_hi) + dot(m_hi, x_lo) + dot(m_lo, x_hi)
                y = term if y is None else y + term
            for p in range(half):
                at = (p, slice(c * small, (c + 1) * small))
                out_ref[at] = acc_ref[at] + folded(y[:, p * width : (p + 1) * width])


def fields_kernel(own_ref, e_ref, out_ref, *, slices):
    width = e_ref.shape[2] // slices
    for n in range(e_ref.shape[0]):
        out_ref[n] = folded(flipped(e_ref[n], owner_of(own_ref), slices)[:, :width])


def assemble_kernel(own_ref, parts_ref, *refs, slices):
    out_ref = refs[-1]
    width = out_ref.shape[2] // slices
    order = reversed_bits(slices)
    for n in range(out_ref.shape[0]):
        pieces = [None] * slices
        for i, p in enumerate(order):
            pieces[p] = unfolded(parts_ref[i, n], width)
        out_ref[n] = flipped(jnp.concatenate(pieces, axis=1), owner_of(own_ref), slices)


def assembled(own, every, shape, begin, onto=()):
    owners, count, small, _ = every.shape
    steps, block, cols = shape
    return pl.pallas_call(
        functools.partial(assemble_kernel, slices=owners),
        grid=(1,),
        in_specs=[smem(), pl.BlockSpec(every.shape, lambda i: (0, 0, 0, 0))] + [pl.BlockSpec(memory_space=pl.ANY)] * len(onto),
        out_specs=pl.BlockSpec((count, block, cols), lambda i: (begin // count, 0, 0)),
        out_shape=jax.ShapeDtypeStruct(shape, F32),
        input_output_aliases={2: 0} if onto else {},
        compiler_params=pltpu.CompilerParams(vmem_limit_bytes=24 << 20),
        cost_estimate=LIGHT,
        name="assemble",
    )(own, every, *onto)


def whole_call(kernel, name, out_shapes, *args, scratch=()):
    vmem = pl.BlockSpec(memory_space=pltpu.VMEM)
    out = [jax.ShapeDtypeStruct(s, F32) for s in out_shapes]
    return pl.pallas_call(
        kernel,
        in_specs=[smem()] + [vmem] * (len(args) - 1),
        out_specs=[vmem] * len(out),
        out_shape=out,
        scratch_shapes=[pltpu.VMEM(s, F32) for s in scratch],
        compiler_params=pltpu.CompilerParams(vmem_limit_bytes=40 << 20),
        cost_estimate=LIGHT,
        name=name,
    )(*args)


def sealed(held, *names):
    names = names or tuple(held)
    held.update(zip(names, lax.optimization_barrier(tuple(held[k] for k in names)), strict=True))


def local(lag_matrices, history, excitation):
    owners, columns = lax.axis_size("lag"), lax.axis_size("col")
    owner, column = lax.axis_index("lag"), lax.axis_index("col")
    lags, rows, block = lag_matrices.shape
    steps, _, cols = excitation.shape
    width = cols // owners
    small = block * width // LANES
    bits = bit_count(owners)
    back = steps - 1
    own = jnp.reshape(owner + (column << PLACE), (1,)).astype(jnp.int32)
    tiles = max(1, rows // 512)
    held = {}

    def stage_pairs(stage):
        def partner(i):
            lag, col = divmod(i, columns)
            if stage < 2:
                return lag * columns + (col ^ 1) if (lag & 1) == stage else (lag ^ 2) * columns + col
            return (lag ^ (1 << stage)) * columns + col

        return [(i, partner(i)) for i in range(owners * columns)]

    def offered(slots):
        return jnp.stack(slots[len(slots) // 2 :])

    def taken(slots, offer, stage):
        got = lax.ppermute(offer, ("lag", "col"), stage_pairs(stage))
        return [slots[i] + got[i] for i in range(len(slots) // 2)]

    def owners_sum(acc):
        for b in range(1, bits):
            half = acc.shape[0] // 2
            got = exchanged(acc[half:], "lag", 1 << b)
            if half == 1:
                return acc[0], got[0]
            acc = acc[:half] + got
        return acc[0], jnp.zeros_like(acc[0])

    def scattered(acc, bit):
        while len(acc) > 4:
            got = exchanged(jnp.stack(acc[1::2]), "col", bit)
            acc = [a + got[i] for i, a in enumerate(acc[0::2])]
            bit *= 2
        return [acc[0]] + [exchanged(acc[d], "col", d * bit) for d in range(1, len(acc))]

    def gathered(x):
        for b in reversed(range(1, bits)):
            x = jnp.concatenate([x, exchanged(x, "lag", 1 << b)], axis=0)
        return x

    def partner_sum(n):
        return held[f"keep{n}"] + exchanged(held[f"send{n}"], "lag", 1)

    def with_tail(n):
        pair = with_carried(own, held["carried"], held[f"keep{n}"], held[f"send{n}"], lag_matrices, n, owners)
        held[f"keep{n}"], held[f"send{n}"] = pair

    newest, tail = staged(own, lag_matrices, history, back)
    top = 1 << (bits - 1)
    held["newest"], held["got"] = newest, lax.ppermute(newest, "lag", [(0, top)])
    held["carried"] = lax.ppermute(tail, "lag", [(i, i + 1) for i in range(owners - 1)])
    partials = bulk(own, history, lag_matrices, steps, owners, tiles)
    for n in range(steps):
        held[f"keep{n}"], held[f"send{n}"] = partials[2 * n : 2 * n + 2]
    held["lag2"], held["lag3"] = partials[-2:]
    sealed(held, "send0", "got", "carried")

    got = exchanged(held["send0"], "lag", 1)
    slots = [held["keep0"][i] + got[i] for i in range(owners)]
    held["offer"] = offered(slots)
    sealed(held, "offer", "keep1", "newest")
    slots = taken(slots, held["offer"], 0)
    with_tail(1)
    held["field"] = whole_call(functools.partial(fields_kernel, slices=owners), "fields", [(steps, small, LANES)], own, excitation)[0]
    newest = jnp.where((owner & top) != 0, held["got"], held["newest"])
    for b in reversed(range(1, bits - 1)):
        got = lax.ppermute(newest, "lag", [(i, i + (1 << b)) for i in range(0, owners, 2 << b)])
        newest = jnp.where((owner >> b) & 1 == 1, got, newest)
    held["newest"] = newest
    held["offer"] = offered(slots)
    sealed(held, "offer", "keep1", "send1", "field", "keep2", "newest")
    held["odd"] = lax.ppermute(held["newest"], "lag", [(i, i + 1) for i in range(0, owners, 2)])
    slots = taken(slots, held["offer"], 1)
    for b in range(2, bits):
        slots = taken(slots, offered(slots), b)
    with_tail(2)
    held["past1"] = partner_sum(1)
    held["acc0"] = slots[0]
    sealed(held, "acc0", "keep2", "send2", "keep3", "odd")
    acc = whole_call(merge_kernel, "merge", [(small, LANES)] * (columns // 2), own, held["acc0"])
    parts = scattered(acc, 2)
    held["mine1"], held["got1"] = owners_sum(held["past1"])
    with_tail(3)
    held["past2"] = partner_sum(2)
    held.update((f"part{i}", part) for i, part in enumerate(parts))
    sealed(held, "keep3", "send3", "past2", "lag2", "mine1", "got1", *(f"part{i}" for i in range(len(parts))))
    a, b = held["mine1"], held["got1"]
    parts = [held[f"part{i}"] for i in range(len(parts))]

    shaped = (columns, small, LANES)
    halves = [(columns // 2, small, LANES)] * 2
    shown = []
    for n in range(1, steps):
        x, keep, send = whole_call(
            functools.partial(chain_kernel, width=width), "chain", [(small, LANES), *halves],
            own, held["field"][n - 1], a.reshape(shaped), b.reshape(shaped), held["newest"], held["odd"], *parts,
        )
        if n + 1 < steps:
            if n == 1:
                held["x"] = x
                sealed(held, "x", "lag2", "send3")
                x = held["x"]
                held["past3"] = partner_sum(3)
            else:
                held["x"] = x
                sealed(held, "x", "lag3", "past3")
                x = held["x"]
            held[f"odd{n + 1}"] = lax.ppermute(held[f"lag{n + 1}"], "lag", [(0, 1)])
            shown.append(gathered(x[None]))
            terms = [v for k in range(2, n + 2) for v in (held[f"lag{k}"], held[f"odd{k}"], shown[n + 1 - k])]
            past = whole_call(
                functools.partial(late_kernel, width=width), "late", [held[f"past{n + 1}"].shape],
                own, held[f"past{n + 1}"], *terms,
            )[0]
            a, b = owners_sum(past)
        else:
            shown.append(gathered(x[None]))
        acc = keep + exchanged(send, "col", 1)
        parts = scattered([acc[i] for i in range(columns // 2)], 2)
    early = jnp.stack(shown, axis=1)
    early = jnp.concatenate([early, exchanged(early, "lag", 1)], axis=0)
    held["dens"] = assembled(own, early, excitation.shape, 0)
    held.update((f"part{i}", part) for i, part in enumerate(parts))
    sealed(held, "dens", *(f"part{i}" for i in range(len(parts))))
    x = held["field"][steps - 1] - functools.reduce(jnp.add, [held[f"part{i}"] for i in range(len(parts))])
    newest = gathered(x[None])
    newest = jnp.concatenate([newest, exchanged(newest, "lag", 1)], axis=0)
    return assembled(own, newest[:, None], excitation.shape, steps - 1, [held["dens"]])


def solution(mesh):
    return jax.shard_map(
        local,
        mesh=mesh,
        in_specs=(P("lag", None, "col"), P("lag", "col", None), P(None, "col", None)),
        out_specs=P(None, "col", None),
        check_vma=False,
    )
```

```python
import functools

import jax
import jax.numpy as jnp
from jax import lax
from jax.experimental import pallas as pl
from jax.experimental.pallas import tpu as pltpu
from jax.sharding import PartitionSpec as P

LANES = 128
BF = jnp.bfloat16
F32 = jnp.float32
PLACE = 16
LIGHT = pl.CostEstimate(flops=1, bytes_accessed=1, transcendentals=0)
KINDS = tuple((outer, inner) for outer in (1, 2, 3) for inner in (1, 2, 3))
MEMBERS = {1: (1,), 2: (0, 1), 3: (0,)}


def swap_pairs(axis, bit):
    return [(i, i ^ bit) for i in range(lax.axis_size(axis))]


def exchanged(value, axis, bit):
    return lax.ppermute(value, axis, swap_pairs(axis, bit))


def bit_count(n):
    return n.bit_length() - 1


def reversed_bits(n):
    bits = bit_count(n)
    return [sum(((i >> b) & 1) << (bits - 1 - b) for b in range(bits)) for i in range(n)]


def owner_of(own_ref):
    return own_ref[0] & ((1 << PLACE) - 1)


def column_of(own_ref):
    return own_ref[0] >> PLACE


def split(v):
    hi = v.astype(BF)
    return hi, (v - hi.astype(F32)).astype(BF)


def dot(a, b):
    return jnp.dot(a, b, preferred_element_type=F32)


def flipped(v, own, slices):
    cols = v.shape[-1]
    width = cols // slices
    for b in range(bit_count(slices)):
        step = width << b
        swapped = jnp.concatenate(
            [v[:, (start ^ step) : (start ^ step) + step] for start in range(0, cols, step)], axis=1
        )
        v = jnp.where(((own >> b) & 1) == 1, swapped, v)
    return v


def folded(v):
    rows, width = v.shape
    parts = LANES // width
    step = rows // parts
    return jnp.concatenate([v[s * step : (s + 1) * step] for s in range(parts)], axis=1) if parts > 1 else v


def unfolded(v, width):
    parts = LANES // width
    return jnp.concatenate([v[:, s * width : (s + 1) * width] for s in range(parts)], axis=0) if parts > 1 else v


def source_sums(get, outer, inner, base):
    def along(inner_offset):
        if outer == 1:
            return get(base + 2 + inner_offset) - get(base + inner_offset)
        if outer == 2:
            return get(base + inner_offset)
        return get(base + inner_offset) - get(base - 2 + inner_offset)

    if inner == 1:
        return along(1) - along(0)
    if inner == 2:
        return along(0)
    return along(0) - along(-1)


def prepare_sources(kinds, get, ready, own, slices, groups, hi_ref, lo_ref):
    block = hi_ref.shape[1] // groups
    for g in range(groups):
        ready(g)
        for i, (outer, inner) in enumerate(kinds):
            hi, lo = split(flipped(source_sums(get, outer, inner, 4 * g), own, slices))
            hi_ref[i, g * block : (g + 1) * block, :] = hi
            lo_ref[i, g * block : (g + 1) * block, :] = lo


def write_folded(y, block, keep_ref, send_ref, slices):
    width = y.shape[1] // slices
    small = block * width // LANES
    half = slices // 2
    for b in range(y.shape[0] // block):
        rows = y[b * block : (b + 1) * block]
        for i, p in enumerate(reversed_bits(slices)):
            piece = folded(rows[:, p * width : (p + 1) * width])
            (send_ref if i // half else keep_ref)[i % half, b * small : (b + 1) * small, :] = piece


def slot(core, x_part, y_part, half):
    top, low = y_part // (half // 2), y_part % (half // 2)
    return jnp.where(core == 0, (x_part * 2 + top) * (half // 2) + low, (top * 2 + x_part) * (half // 2) + low)


def write_slots(y, block, own_ref, keep_ref, send_ref, slices):
    width = y.shape[1] // slices
    half = slices // 2
    core, side = owner_of(own_ref) & 1, column_of(own_ref) & 1
    for b in range(y.shape[0] // block):
        rows = y[b * block : (b + 1) * block]
        for i, p in enumerate(reversed_bits(slices)):
            piece = folded(rows[:, p * width : (p + 1) * width])
            at = slot(core ^ (i // half), (b & 1) ^ side, i % half, half)
            (send_ref if i // half else keep_ref)[at, b // 2, :, :] = piece


def products(kinds, a_ref, hi_ref, lo_ref):
    groups = a_ref.shape[0]
    out = []
    for i, (outer, inner) in enumerate(kinds):
        his, los = [], []
        for g in range(groups):
            total = None
            for u in MEMBERS[outer]:
                for v in MEMBERS[inner]:
                    term = a_ref[g, u, v]
                    total = term if total is None else total + term
            hi, lo = split(total)
            his.append(hi)
            los.append(lo)
        hi, lo = jnp.concatenate(his, axis=1), jnp.concatenate(los, axis=1)
        out.append(dot(hi, hi_ref[i]) + dot(hi, lo_ref[i]) + dot(lo, hi_ref[i]))
    return out


def bulk_kernel(own_ref, history_ref, a_ref, *refs, slices, block):
    outs, (second_ref, third_ref, hi_ref, lo_ref, tiles_ref, past_ref, sems, past_sems) = refs[:-8], refs[-8:]
    step, steps = pl.program_id(0), pl.num_programs(0)
    tile = tiles_ref.shape[4]

    def fetch(i):
        rows = pl.ds(pl.multiple_of(i * tile, tile), tile)
        return pltpu.make_async_copy(a_ref.at[:, :, :, rows, :], tiles_ref.at[i % 2], sems.at[i % 2])

    def fetch_past(g):
        lags = pl.ds(4 * g, 4)
        return pltpu.make_async_copy(history_ref.at[lags], past_ref.at[lags], past_sems.at[g])

    @pl.when(step == 0)
    def _():
        for g in range(a_ref.shape[0]):
            fetch_past(g).start()
        fetch(0).start()

    @pl.when(step == 0)
    def _():
        def get(i):
            return past_ref[i] if i >= 0 else jnp.zeros(past_ref.shape[1:], F32)

        prepare_sources(KINDS, get, lambda g: fetch_past(g).wait(), owner_of(own_ref), slices, a_ref.shape[0], hi_ref, lo_ref)

    fetch(step).wait()

    @pl.when(step + 1 < steps)
    def _():
        fetch(step + 1).start()

    a_ref = tiles_ref.at[step % 2]
    second_ref[...] = a_ref[0, 0, 1]
    third_ref[...] = a_ref[0, 1, 0]
    p11, p12, p13, p21, p22, p23, p31, p32, p33 = products(KINDS, a_ref, hi_ref, lo_ref)
    write_slots((p12 + p22) + (p11 + p21), block, own_ref, outs[0], outs[1], slices)
    times = ((p12 + p22) - (p13 + p23), (p21 + p22) - (p31 + p32), (p22 - p23) - (p32 - p33))
    for n, y in enumerate(times):
        write_folded(y, block, outs[2 * n + 2], outs[2 * n + 3], slices)


def carried_kernel(own_ref, tail_ref, keep_in, send_in, *refs, slices):
    matrices, (keep_ref, send_ref) = refs[:-2], refs[-2:]
    back, block = tail_ref.shape[:2]
    count = len(matrices)
    width = tail_ref.shape[2] // slices
    small = block * width // LANES
    half = slices // 2
    x = jnp.concatenate([flipped(tail_ref[back - count + j], owner_of(own_ref), slices) for j in range(count)], axis=0)
    x_hi, x_lo = split(x)
    for c in range(matrices[0].shape[1] // block):
        m_hi, m_lo = split(jnp.concatenate([r[0, c * block : (c + 1) * block, :] for r in matrices], axis=1))
        y = dot(m_hi, x_hi) + dot(m_hi, x_lo) + dot(m_lo, x_hi)
        for i, p in enumerate(reversed_bits(slices)):
            at = (i % half, slice(c * small, (c + 1) * small))
            from_ref, to_ref = (send_in, send_ref) if i // half else (keep_in, keep_ref)
            to_ref[at] = from_ref[at] + folded(y[:, p * width : (p + 1) * width])


def with_carried(own, tail, keep, send, matrices, count, slices):
    lags, rows, block = matrices.shape
    return pl.pallas_call(
        functools.partial(carried_kernel, slices=slices),
        grid=(1,),
        in_specs=[smem()]
        + [pl.BlockSpec(v.shape, lambda i: (0, 0, 0)) for v in (tail, keep, send)]
        + [pl.BlockSpec((1, rows, block), lambda i, j=j: (j, 0, 0)) for j in range(count)],
        out_specs=[pl.BlockSpec(keep.shape, lambda i: (0, 0, 0))] * 2,
        out_shape=[jax.ShapeDtypeStruct(keep.shape, F32)] * 2,
        compiler_params=pltpu.CompilerParams(vmem_limit_bytes=40 << 20),
        cost_estimate=LIGHT,
        name="carried",
    )(own, tail, keep, send, *[matrices] * count)


def smem():
    return pl.BlockSpec(memory_space=pltpu.SMEM)


def bulk(own, history, matrices, steps, slices, tiles):
    lags, rows, block = matrices.shape
    cols = history.shape[2]
    groups = lags // 4
    tile = rows // tiles
    small = block * (cols // slices) // LANES
    pairs = rows // block // 2
    flat = jax.ShapeDtypeStruct((slices // 2, 2 * pairs * small, LANES), F32)
    flat_spec = pl.BlockSpec((slices // 2, 2 * pairs * small // tiles, LANES), lambda i: (0, i, 0))
    slots = jax.ShapeDtypeStruct((slices, pairs, small, LANES), F32)
    slots_spec = pl.BlockSpec((slices, pairs // tiles, small, LANES), lambda i: (0, i, 0, 0))
    return pl.pallas_call(
        functools.partial(bulk_kernel, slices=slices, block=block),
        grid=(tiles,),
        in_specs=[
            smem(),
            pl.BlockSpec(memory_space=pl.ANY),
            pl.BlockSpec(memory_space=pl.ANY),
        ],
        out_specs=[slots_spec] * 2 + [flat_spec] * (2 * steps - 2) + [pl.BlockSpec((tile, block), lambda i: (i, 0))] * 2,
        out_shape=[slots] * 2 + [flat] * (2 * steps - 2) + [jax.ShapeDtypeStruct((rows, block), F32)] * 2,
        scratch_shapes=[
            *[pltpu.VMEM((len(KINDS), groups * block, cols), BF)] * 2,
            pltpu.VMEM((2, groups, 2, 2, tile, block), F32),
            pltpu.VMEM(history.shape, F32),
            pltpu.SemaphoreType.DMA((2,)),
            pltpu.SemaphoreType.DMA((groups,)),
        ],
        compiler_params=pltpu.CompilerParams(vmem_limit_bytes=61 << 20),
        cost_estimate=pl.CostEstimate(
            flops=2 * 4 * len(KINDS) * groups * rows * block * cols,
            bytes_accessed=4 * matrices.size,
            transcendentals=0,
        ),
        name="bulk",
    )(own, history, matrices.reshape(groups, 2, 2, rows, block))


def stage_kernel(own_ref, a_ref, *refs):
    slabs, (newest_ref, tail_ref) = refs[:-2], refs[-2:]
    newest_ref[...] = a_ref[0]
    for i, slab in enumerate(slabs):
        tail_ref[i] = slab[0]


def staged(own, matrices, history, back):
    lags, rows, block = matrices.shape
    cols = history.shape[2]
    shapes = [(rows, block), (back, block, cols)]
    return pl.pallas_call(
        stage_kernel,
        grid=(1,),
        in_specs=[smem(), pl.BlockSpec((1, rows, block), lambda i: (0, 0, 0))]
        + [pl.BlockSpec((1, block, cols), lambda i, at=lags - back + k: (at, 0, 0)) for k in range(back)],
        out_specs=[pl.BlockSpec(s, lambda i, r=len(s): (0,) * r) for s in shapes],
        out_shape=[jax.ShapeDtypeStruct(s, F32) for s in shapes],
        compiler_params=pltpu.CompilerParams(vmem_limit_bytes=61 << 20),
        cost_estimate=LIGHT,
        name="stage",
    )(own, matrices, *[history] * back)


def merge_kernel(own_ref, a_ref, *out_refs):
    for d, out_ref in enumerate(out_refs):
        out_ref[...] = a_ref[(column_of(own_ref) >> 1) ^ d]


def chain_kernel(own_ref, e_ref, a_ref, b_ref, m_ref, got_ref, *refs, width):
    parts, (x_ref, keep_ref, send_ref) = refs[:-3], refs[-3:]
    core, own = owner_of(own_ref) & 1, column_of(own_ref)
    total = parts[0][...]
    for part in parts[1:]:
        total = total + part[...]
    x = e_ref[...] - total
    x_ref[...] = x
    block = m_ref.shape[1]
    x_hi, x_lo = split(unfolded(x, width))
    x_both = jnp.concatenate([x_hi, x_lo], axis=1)
    for q in range(a_ref.shape[0]):
        c = own ^ q
        at = pl.ds(pl.multiple_of(c * block, block), block)
        m_hi, m_lo = split(jnp.where(core == 1, got_ref[at, :], m_ref[at, :]))
        both = dot(m_hi, x_both)
        y = both[:, :width] + both[:, width:] + dot(m_lo, x_hi)
        (send_ref if q % 2 else keep_ref)[q // 2] = folded(y) + (a_ref[c] + b_ref[c])


def late_kernel(own_ref, acc_ref, *refs, width):
    out_ref, terms = refs[-1], [refs[i : i + 3] for i in range(0, len(refs) - 1, 3)]
    half = acc_ref.shape[0]

    @pl.when(owner_of(own_ref) >= 2)
    def _():
        out_ref[...] = acc_ref[...]

    @pl.when(owner_of(own_ref) < 2)
    def _():
        rows, block = terms[0][0].shape
        small = block * width // LANES
        sources = [split(jnp.concatenate([unfolded(r[p], width) for p in range(half)], axis=1)) for _, _, r in terms]
        for c in range(rows // block):
            y = None
            at = slice(c * block, (c + 1) * block)
            for (mine_ref, got_ref, _), (x_hi, x_lo) in zip(terms, sources, strict=True):
                m_hi, m_lo = split(jnp.where((owner_of(own_ref) & 1) == 1, got_ref[at], mine_ref[at]))
                term = dot(m_hi, x_hi) + dot(m_hi, x_lo) + dot(m_lo, x_hi)
                y = term if y is None else y + term
            for p in range(half):
                at = (p, slice(c * small, (c + 1) * small))
                out_ref[at] = acc_ref[at] + folded(y[:, p * width : (p + 1) * width])


def fields_kernel(own_ref, e_ref, out_ref, *, slices):
    width = e_ref.shape[2] // slices
    for n in range(e_ref.shape[0]):
        out_ref[n] = folded(flipped(e_ref[n], owner_of(own_ref), slices)[:, :width])


def assemble_kernel(own_ref, parts_ref, *refs, slices):
    out_ref = refs[-1]
    width = out_ref.shape[2] // slices
    order = reversed_bits(slices)
    for n in range(out_ref.shape[0]):
        pieces = [None] * slices
        for i, p in enumerate(order):
            pieces[p] = unfolded(parts_ref[i, n], width)
        out_ref[n] = flipped(jnp.concatenate(pieces, axis=1), owner_of(own_ref), slices)


def assembled(own, every, shape, begin, onto=()):
    owners, count, small, _ = every.shape
    steps, block, cols = shape
    return pl.pallas_call(
        functools.partial(assemble_kernel, slices=owners),
        grid=(1,),
        in_specs=[smem(), pl.BlockSpec(every.shape, lambda i: (0, 0, 0, 0))] + [pl.BlockSpec(memory_space=pl.ANY)] * len(onto),
        out_specs=pl.BlockSpec((count, block, cols), lambda i: (begin // count, 0, 0)),
        out_shape=jax.ShapeDtypeStruct(shape, F32),
        input_output_aliases={2: 0} if onto else {},
        compiler_params=pltpu.CompilerParams(vmem_limit_bytes=24 << 20),
        cost_estimate=LIGHT,
        name="assemble",
    )(own, every, *onto)


def whole_call(kernel, name, out_shapes, *args, scratch=()):
    vmem = pl.BlockSpec(memory_space=pltpu.VMEM)
    out = [jax.ShapeDtypeStruct(s, F32) for s in out_shapes]
    return pl.pallas_call(
        kernel,
        in_specs=[smem()] + [vmem] * (len(args) - 1),
        out_specs=[vmem] * len(out),
        out_shape=out,
        scratch_shapes=[pltpu.VMEM(s, F32) for s in scratch],
        compiler_params=pltpu.CompilerParams(vmem_limit_bytes=40 << 20),
        cost_estimate=LIGHT,
        name=name,
    )(*args)


def sealed(held, *names):
    names = names or tuple(held)
    held.update(zip(names, lax.optimization_barrier(tuple(held[k] for k in names)), strict=True))


def local(lag_matrices, history, excitation):
    owners, columns = lax.axis_size("lag"), lax.axis_size("col")
    owner, column = lax.axis_index("lag"), lax.axis_index("col")
    lags, rows, block = lag_matrices.shape
    steps, _, cols = excitation.shape
    width = cols // owners
    small = block * width // LANES
    bits = bit_count(owners)
    back = steps - 1
    own = jnp.reshape(owner + (column << PLACE), (1,)).astype(jnp.int32)
    tiles = max(1, rows // 512)
    held = {}

    def stage_pairs(stage):
        def partner(i):
            lag, col = divmod(i, columns)
            if stage < 2:
                return lag * columns + (col ^ 1) if (lag & 1) == stage else (lag ^ 2) * columns + col
            return (lag ^ (1 << stage)) * columns + col

        return [(i, partner(i)) for i in range(owners * columns)]

    def offered(slots):
        return jnp.stack(slots[len(slots) // 2 :])

    def taken(slots, offer, stage):
        got = lax.ppermute(offer, ("lag", "col"), stage_pairs(stage))
        return [slots[i] + got[i] for i in range(len(slots) // 2)]

    def owners_sum(acc):
        for b in range(1, bits):
            half = acc.shape[0] // 2
            got = exchanged(acc[half:], "lag", 1 << b)
            if half == 1:
                return acc[0], got[0]
            acc = acc[:half] + got
        return acc[0], jnp.zeros_like(acc[0])

    def scattered(acc, bit):
        while len(acc) > 4:
            got = exchanged(jnp.stack(acc[1::2]), "col", bit)
            acc = [a + got[i] for i, a in enumerate(acc[0::2])]
            bit *= 2
        return [acc[0]] + [exchanged(acc[d], "col", d * bit) for d in range(1, len(acc))]

    def gathered(x):
        for b in reversed(range(1, bits)):
            x = jnp.concatenate([x, exchanged(x, "lag", 1 << b)], axis=0)
        return x

    def partner_sum(n):
        return held[f"keep{n}"] + exchanged(held[f"send{n}"], "lag", 1)

    def with_tail(n):
        pair = with_carried(own, held["carried"], held[f"keep{n}"], held[f"send{n}"], lag_matrices, n, owners)
        held[f"keep{n}"], held[f"send{n}"] = pair

    newest, tail = staged(own, lag_matrices, history, back)
    top = 1 << (bits - 1)
    held["newest"], held["got"] = newest, lax.ppermute(newest, "lag", [(0, top)])
    held["carried"] = lax.ppermute(tail, "lag", [(i, i + 1) for i in range(owners - 1)])
    partials = bulk(own, history, lag_matrices, steps, owners, tiles)
    for n in range(steps):
        held[f"keep{n}"], held[f"send{n}"] = partials[2 * n : 2 * n + 2]
    held["lag2"], held["lag3"] = partials[-2:]
    sealed(held, "send0", "got", "carried")

    got = exchanged(held["send0"], "lag", 1)
    slots = [held["keep0"][i] + got[i] for i in range(owners)]
    held["offer"] = offered(slots)
    sealed(held, "offer", "keep1", "newest")
    slots = taken(slots, held["offer"], 0)
    with_tail(1)
    held["field"] = whole_call(functools.partial(fields_kernel, slices=owners), "fields", [(steps, small, LANES)], own, excitation)[0]
    newest = jnp.where((owner & top) != 0, held["got"], held["newest"])
    for b in reversed(range(1, bits - 1)):
        got = lax.ppermute(newest, "lag", [(i, i + (1 << b)) for i in range(0, owners, 2 << b)])
        newest = jnp.where((owner >> b) & 1 == 1, got, newest)
    held["newest"] = newest
    held["offer"] = offered(slots)
    sealed(held, "offer", "keep1", "send1", "field", "keep2", "newest")
    held["odd"] = lax.ppermute(held["newest"], "lag", [(i, i + 1) for i in range(0, owners, 2)])
    slots = taken(slots, held["offer"], 1)
    for b in range(2, bits):
        slots = taken(slots, offered(slots), b)
    with_tail(2)
    held["past1"] = partner_sum(1)
    held["acc0"] = slots[0]
    sealed(held, "acc0", "keep2", "send2", "keep3", "odd")
    acc = whole_call(merge_kernel, "merge", [(small, LANES)] * (columns // 2), own, held["acc0"])
    parts = scattered(acc, 2)
    held["mine1"], held["got1"] = owners_sum(held["past1"])
    with_tail(3)
    held["past2"] = partner_sum(2)
    held.update((f"part{i}", part) for i, part in enumerate(parts))
    sealed(held, "keep3", "send3", "past2", "lag2", "mine1", "got1", *(f"part{i}" for i in range(len(parts))))
    a, b = held["mine1"], held["got1"]
    parts = [held[f"part{i}"] for i in range(len(parts))]

    shaped = (columns, small, LANES)
    halves = [(columns // 2, small, LANES)] * 2
    shown = []
    for n in range(1, steps):
        x, keep, send = whole_call(
            functools.partial(chain_kernel, width=width), "chain", [(small, LANES), *halves],
            own, held["field"][n - 1], a.reshape(shaped), b.reshape(shaped), held["newest"], held["odd"], *parts,
        )
        if n + 1 < steps:
            if n == 1:
                held["x"] = x
                sealed(held, "x", "lag2", "send3")
                x = held["x"]
                held["past3"] = partner_sum(3)
            else:
                held["x"] = x
                sealed(held, "x", "lag3", "past3")
                x = held["x"]
            held[f"odd{n + 1}"] = lax.ppermute(held[f"lag{n + 1}"], "lag", [(0, 1)])
            shown.append(gathered(x[None]))
            terms = [v for k in range(2, n + 2) for v in (held[f"lag{k}"], held[f"odd{k}"], shown[n + 1 - k])]
            past = whole_call(
                functools.partial(late_kernel, width=width), "late", [held[f"past{n + 1}"].shape],
                own, held[f"past{n + 1}"], *terms,
            )[0]
            a, b = owners_sum(past)
        else:
            shown.append(gathered(x[None]))
        acc = keep + exchanged(send, "col", 1)
        parts = scattered([acc[i] for i in range(columns // 2)], 2)
    early = jnp.stack(shown, axis=1)
    early = jnp.concatenate([early, exchanged(early, "lag", 1)], axis=0)
    held["dens"] = assembled(own, early, excitation.shape, 0)
    held.update((f"part{i}", part) for i, part in enumerate(parts))
    sealed(held, "dens", *(f"part{i}" for i in range(len(parts))))
    x = held["field"][steps - 1] - functools.reduce(jnp.add, [held[f"part{i}"] for i in range(len(parts))])
    newest = gathered(x[None])
    newest = jnp.concatenate([newest, exchanged(newest, "lag", 1)], axis=0)
    return assembled(own, newest[:, None], excitation.shape, steps - 1, [held["dens"]])


def solution(mesh):
    return jax.shard_map(
        local,
        mesh=mesh,
        in_specs=(P("lag", None, "col"), P("lag", "col", None), P(None, "col", None)),
        out_specs=P(None, "col", None),
        check_vma=False,
    )
```

```python
import functools

import jax
import jax.numpy as jnp
from jax import lax
from jax.experimental import pallas as pl
from jax.experimental.pallas import tpu as pltpu
from jax.sharding import PartitionSpec as P

LANES = 128
BF = jnp.bfloat16
F32 = jnp.float32
PLACE = 16
LIGHT = pl.CostEstimate(flops=1, bytes_accessed=1, transcendentals=0)
KINDS = tuple((outer, inner) for outer in (1, 2, 3) for inner in (1, 2, 3))
MEMBERS = {1: (1,), 2: (0, 1), 3: (0,)}


def swap_pairs(axis, bit):
    return [(i, i ^ bit) for i in range(lax.axis_size(axis))]


def exchanged(value, axis, bit):
    return lax.ppermute(value, axis, swap_pairs(axis, bit))


def bit_count(n):
    return n.bit_length() - 1


def reversed_bits(n):
    bits = bit_count(n)
    return [sum(((i >> b) & 1) << (bits - 1 - b) for b in range(bits)) for i in range(n)]


def owner_of(own_ref):
    return own_ref[0] & ((1 << PLACE) - 1)


def column_of(own_ref):
    return own_ref[0] >> PLACE


def split(v):
    hi = v.astype(BF)
    return hi, (v - hi.astype(F32)).astype(BF)


def dot(a, b):
    return jnp.dot(a, b, preferred_element_type=F32)


def flipped(v, own, slices):
    cols = v.shape[-1]
    width = cols // slices
    for b in range(bit_count(slices)):
        step = width << b
        swapped = jnp.concatenate(
            [v[:, (start ^ step) : (start ^ step) + step] for start in range(0, cols, step)], axis=1
        )
        v = jnp.where(((own >> b) & 1) == 1, swapped, v)
    return v


def folded(v):
    rows, width = v.shape
    parts = LANES // width
    step = rows // parts
    return jnp.concatenate([v[s * step : (s + 1) * step] for s in range(parts)], axis=1) if parts > 1 else v


def unfolded(v, width):
    parts = LANES // width
    return jnp.concatenate([v[:, s * width : (s + 1) * width] for s in range(parts)], axis=0) if parts > 1 else v


def source_sums(get, outer, inner, base):
    def along(inner_offset):
        if outer == 1:
            return get(base + 2 + inner_offset) - get(base + inner_offset)
        if outer == 2:
            return get(base + inner_offset)
        return get(base + inner_offset) - get(base - 2 + inner_offset)

    if inner == 1:
        return along(1) - along(0)
    if inner == 2:
        return along(0)
    return along(0) - along(-1)


def prepare_sources(kinds, get, ready, own, slices, groups, hi_ref, lo_ref):
    block = hi_ref.shape[1] // groups
    for g in range(groups):
        ready(g)
        for i, (outer, inner) in enumerate(kinds):
            hi, lo = split(flipped(source_sums(get, outer, inner, 4 * g), own, slices))
            hi_ref[i, g * block : (g + 1) * block, :] = hi
            lo_ref[i, g * block : (g + 1) * block, :] = lo


def write_folded(y, block, keep_ref, send_ref, slices):
    width = y.shape[1] // slices
    small = block * width // LANES
    half = slices // 2
    for b in range(y.shape[0] // block):
        rows = y[b * block : (b + 1) * block]
        for i, p in enumerate(reversed_bits(slices)):
            piece = folded(rows[:, p * width : (p + 1) * width])
            (send_ref if i // half else keep_ref)[i % half, b * small : (b + 1) * small, :] = piece


def slot(core, x_part, y_part, half):
    top, low = y_part // (half // 2), y_part % (half // 2)
    return jnp.where(core == 0, (x_part * 2 + top) * (half // 2) + low, (top * 2 + x_part) * (half // 2) + low)


def write_slots(y, block, own_ref, keep_ref, send_ref, slices):
    width = y.shape[1] // slices
    half = slices // 2
    core, side = owner_of(own_ref) & 1, column_of(own_ref) & 1
    for b in range(y.shape[0] // block):
        rows = y[b * block : (b + 1) * block]
        for i, p in enumerate(reversed_bits(slices)):
            piece = folded(rows[:, p * width : (p + 1) * width])
            at = slot(core ^ (i // half), (b & 1) ^ side, i % half, half)
            (send_ref if i // half else keep_ref)[at, b // 2, :, :] = piece


def products(kinds, a_ref, hi_ref, lo_ref):
    groups = a_ref.shape[0]
    out = []
    for i, (outer, inner) in enumerate(kinds):
        his, los = [], []
        for g in range(groups):
            total = None
            for u in MEMBERS[outer]:
                for v in MEMBERS[inner]:
                    term = a_ref[g, u, v]
                    total = term if total is None else total + term
            hi, lo = split(total)
            his.append(hi)
            los.append(lo)
        hi, lo = jnp.concatenate(his, axis=1), jnp.concatenate(los, axis=1)
        out.append(dot(hi, hi_ref[i]) + dot(hi, lo_ref[i]) + dot(lo, hi_ref[i]))
    return out


def bulk_kernel(own_ref, history_ref, a_ref, *refs, slices, block):
    outs, (second_ref, third_ref, hi_ref, lo_ref, tiles_ref, past_ref, sems, past_sems) = refs[:-8], refs[-8:]
    step, steps = pl.program_id(0), pl.num_programs(0)
    tile = tiles_ref.shape[4]

    def fetch(i):
        rows = pl.ds(pl.multiple_of(i * tile, tile), tile)
        return pltpu.make_async_copy(a_ref.at[:, :, :, rows, :], tiles_ref.at[i % 2], sems.at[i % 2])

    def fetch_past(g):
        lags = pl.ds(4 * g, 4)
        return pltpu.make_async_copy(history_ref.at[lags], past_ref.at[lags], past_sems.at[g])

    @pl.when(step == 0)
    def _():
        for g in range(a_ref.shape[0]):
            fetch_past(g).start()
        fetch(0).start()

    @pl.when(step == 0)
    def _():
        def get(i):
            return past_ref[i] if i >= 0 else jnp.zeros(past_ref.shape[1:], F32)

        prepare_sources(KINDS, get, lambda g: fetch_past(g).wait(), owner_of(own_ref), slices, a_ref.shape[0], hi_ref, lo_ref)

    fetch(step).wait()

    @pl.when(step + 1 < steps)
    def _():
        fetch(step + 1).start()

    a_ref = tiles_ref.at[step % 2]
    second_ref[...] = a_ref[0, 0, 1]
    third_ref[...] = a_ref[0, 1, 0]
    p11, p12, p13, p21, p22, p23, p31, p32, p33 = products(KINDS, a_ref, hi_ref, lo_ref)
    write_slots((p12 + p22) + (p11 + p21), block, own_ref, outs[0], outs[1], slices)
    times = ((p12 + p22) - (p13 + p23), (p21 + p22) - (p31 + p32), (p22 - p23) - (p32 - p33))
    for n, y in enumerate(times):
        write_folded(y, block, outs[2 * n + 2], outs[2 * n + 3], slices)


def carried_kernel(own_ref, tail_ref, keep_in, send_in, *refs, slices):
    matrices, (keep_ref, send_ref) = refs[:-2], refs[-2:]
    back, block = tail_ref.shape[:2]
    count = len(matrices)
    width = tail_ref.shape[2] // slices
    small = block * width // LANES
    half = slices // 2
    x = jnp.concatenate([flipped(tail_ref[back - count + j], owner_of(own_ref), slices) for j in range(count)], axis=0)
    x_hi, x_lo = split(x)
    for c in range(matrices[0].shape[1] // block):
        m_hi, m_lo = split(jnp.concatenate([r[0, c * block : (c + 1) * block, :] for r in matrices], axis=1))
        y = dot(m_hi, x_hi) + dot(m_hi, x_lo) + dot(m_lo, x_hi)
        for i, p in enumerate(reversed_bits(slices)):
            at = (i % half, slice(c * small, (c + 1) * small))
            from_ref, to_ref = (send_in, send_ref) if i // half else (keep_in, keep_ref)
            to_ref[at] = from_ref[at] + folded(y[:, p * width : (p + 1) * width])


def with_carried(own, tail, keep, send, matrices, count, slices):
    lags, rows, block = matrices.shape
    return pl.pallas_call(
        functools.partial(carried_kernel, slices=slices),
        grid=(1,),
        in_specs=[smem()]
        + [pl.BlockSpec(v.shape, lambda i: (0, 0, 0)) for v in (tail, keep, send)]
        + [pl.BlockSpec((1, rows, block), lambda i, j=j: (j, 0, 0)) for j in range(count)],
        out_specs=[pl.BlockSpec(keep.shape, lambda i: (0, 0, 0))] * 2,
        out_shape=[jax.ShapeDtypeStruct(keep.shape, F32)] * 2,
        compiler_params=pltpu.CompilerParams(vmem_limit_bytes=40 << 20),
        cost_estimate=LIGHT,
        name="carried",
    )(own, tail, keep, send, *[matrices] * count)


def smem():
    return pl.BlockSpec(memory_space=pltpu.SMEM)


def bulk(own, history, matrices, steps, slices, tiles):
    lags, rows, block = matrices.shape
    cols = history.shape[2]
    groups = lags // 4
    tile = rows // tiles
    small = block * (cols // slices) // LANES
    pairs = rows // block // 2
    flat = jax.ShapeDtypeStruct((slices // 2, 2 * pairs * small, LANES), F32)
    flat_spec = pl.BlockSpec((slices // 2, 2 * pairs * small // tiles, LANES), lambda i: (0, i, 0))
    slots = jax.ShapeDtypeStruct((slices, pairs, small, LANES), F32)
    slots_spec = pl.BlockSpec((slices, pairs // tiles, small, LANES), lambda i: (0, i, 0, 0))
    return pl.pallas_call(
        functools.partial(bulk_kernel, slices=slices, block=block),
        grid=(tiles,),
        in_specs=[
            smem(),
            pl.BlockSpec(memory_space=pl.ANY),
            pl.BlockSpec(memory_space=pl.ANY),
        ],
        out_specs=[slots_spec] * 2 + [flat_spec] * (2 * steps - 2) + [pl.BlockSpec((tile, block), lambda i: (i, 0))] * 2,
        out_shape=[slots] * 2 + [flat] * (2 * steps - 2) + [jax.ShapeDtypeStruct((rows, block), F32)] * 2,
        scratch_shapes=[
            *[pltpu.VMEM((len(KINDS), groups * block, cols), BF)] * 2,
            pltpu.VMEM((2, groups, 2, 2, tile, block), F32),
            pltpu.VMEM(history.shape, F32),
            pltpu.SemaphoreType.DMA((2,)),
            pltpu.SemaphoreType.DMA((groups,)),
        ],
        compiler_params=pltpu.CompilerParams(vmem_limit_bytes=61 << 20),
        cost_estimate=pl.CostEstimate(
            flops=2 * 4 * len(KINDS) * groups * rows * block * cols,
            bytes_accessed=4 * matrices.size,
            transcendentals=0,
        ),
        name="bulk",
    )(own, history, matrices.reshape(groups, 2, 2, rows, block))


def stage_kernel(own_ref, a_ref, *refs):
    slabs, (newest_ref, tail_ref) = refs[:-2], refs[-2:]
    newest_ref[...] = a_ref[0]
    for i, slab in enumerate(slabs):
        tail_ref[i] = slab[0]


def staged(own, matrices, history, back):
    lags, rows, block = matrices.shape
    cols = history.shape[2]
    shapes = [(rows, block), (back, block, cols)]
    return pl.pallas_call(
        stage_kernel,
        grid=(1,),
        in_specs=[smem(), pl.BlockSpec((1, rows, block), lambda i: (0, 0, 0))]
        + [pl.BlockSpec((1, block, cols), lambda i, at=lags - back + k: (at, 0, 0)) for k in range(back)],
        out_specs=[pl.BlockSpec(s, lambda i, r=len(s): (0,) * r) for s in shapes],
        out_shape=[jax.ShapeDtypeStruct(s, F32) for s in shapes],
        compiler_params=pltpu.CompilerParams(vmem_limit_bytes=61 << 20),
        cost_estimate=LIGHT,
        name="stage",
    )(own, matrices, *[history] * back)


def merge_kernel(own_ref, a_ref, *out_refs):
    for d, out_ref in enumerate(out_refs):
        out_ref[...] = a_ref[(column_of(own_ref) >> 1) ^ d]


def chain_kernel(own_ref, e_ref, a_ref, b_ref, m_ref, got_ref, *refs, width):
    parts, (x_ref, keep_ref, send_ref) = refs[:-3], refs[-3:]
    core, own = owner_of(own_ref) & 1, column_of(own_ref)
    total = parts[0][...]
    for part in parts[1:]:
        total = total + part[...]
    x = e_ref[...] - total
    x_ref[...] = x
    block = m_ref.shape[1]
    x_hi, x_lo = split(unfolded(x, width))
    x_both = jnp.concatenate([x_hi, x_lo], axis=1)
    for q in range(a_ref.shape[0]):
        c = own ^ q
        at = pl.ds(pl.multiple_of(c * block, block), block)
        m_hi, m_lo = split(jnp.where(core == 1, got_ref[at, :], m_ref[at, :]))
        both = dot(m_hi, x_both)
        y = both[:, :width] + both[:, width:] + dot(m_lo, x_hi)
        (send_ref if q % 2 else keep_ref)[q // 2] = folded(y) + (a_ref[c] + b_ref[c])


def late_kernel(own_ref, acc_ref, *refs, width):
    out_ref, terms = refs[-1], [refs[i : i + 3] for i in range(0, len(refs) - 1, 3)]
    half = acc_ref.shape[0]

    @pl.when(owner_of(own_ref) >= 2)
    def _():
        out_ref[...] = acc_ref[...]

    @pl.when(owner_of(own_ref) < 2)
    def _():
        rows, block = terms[0][0].shape
        small = block * width // LANES
        sources = [split(jnp.concatenate([unfolded(r[p], width) for p in range(half)], axis=1)) for _, _, r in terms]
        for c in range(rows // block):
            y = None
            at = slice(c * block, (c + 1) * block)
            for (mine_ref, got_ref, _), (x_hi, x_lo) in zip(terms, sources, strict=True):
                m_hi, m_lo = split(jnp.where((owner_of(own_ref) & 1) == 1, got_ref[at], mine_ref[at]))
                term = dot(m_hi, x_hi) + dot(m_hi, x_lo) + dot(m_lo, x_hi)
                y = term if y is None else y + term
            for p in range(half):
                at = (p, slice(c * small, (c + 1) * small))
                out_ref[at] = acc_ref[at] + folded(y[:, p * width : (p + 1) * width])


def fields_kernel(own_ref, e_ref, out_ref, *, slices):
    width = e_ref.shape[2] // slices
    for n in range(e_ref.shape[0]):
        out_ref[n] = folded(flipped(e_ref[n], owner_of(own_ref), slices)[:, :width])


def assemble_kernel(own_ref, parts_ref, *refs, slices):
    out_ref = refs[-1]
    width = out_ref.shape[2] // slices
    order = reversed_bits(slices)
    for n in range(out_ref.shape[0]):
        pieces = [None] * slices
        for i, p in enumerate(order):
            pieces[p] = unfolded(parts_ref[i, n], width)
        out_ref[n] = flipped(jnp.concatenate(pieces, axis=1), owner_of(own_ref), slices)


def assembled(own, every, shape, begin, onto=()):
    owners, count, small, _ = every.shape
    steps, block, cols = shape
    return pl.pallas_call(
        functools.partial(assemble_kernel, slices=owners),
        grid=(1,),
        in_specs=[smem(), pl.BlockSpec(every.shape, lambda i: (0, 0, 0, 0))] + [pl.BlockSpec(memory_space=pl.ANY)] * len(onto),
        out_specs=pl.BlockSpec((count, block, cols), lambda i: (begin // count, 0, 0)),
        out_shape=jax.ShapeDtypeStruct(shape, F32),
        input_output_aliases={2: 0} if onto else {},
        compiler_params=pltpu.CompilerParams(vmem_limit_bytes=24 << 20),
        cost_estimate=LIGHT,
        name="assemble",
    )(own, every, *onto)


def whole_call(kernel, name, out_shapes, *args, scratch=()):
    vmem = pl.BlockSpec(memory_space=pltpu.VMEM)
    out = [jax.ShapeDtypeStruct(s, F32) for s in out_shapes]
    return pl.pallas_call(
        kernel,
        in_specs=[smem()] + [vmem] * (len(args) - 1),
        out_specs=[vmem] * len(out),
        out_shape=out,
        scratch_shapes=[pltpu.VMEM(s, F32) for s in scratch],
        compiler_params=pltpu.CompilerParams(vmem_limit_bytes=40 << 20),
        cost_estimate=LIGHT,
        name=name,
    )(*args)


def sealed(held, *names):
    names = names or tuple(held)
    held.update(zip(names, lax.optimization_barrier(tuple(held[k] for k in names)), strict=True))


def local(lag_matrices, history, excitation):
    owners, columns = lax.axis_size("lag"), lax.axis_size("col")
    owner, column = lax.axis_index("lag"), lax.axis_index("col")
    lags, rows, block = lag_matrices.shape
    steps, _, cols = excitation.shape
    width = cols // owners
    small = block * width // LANES
    bits = bit_count(owners)
    back = steps - 1
    own = jnp.reshape(owner + (column << PLACE), (1,)).astype(jnp.int32)
    tiles = max(1, rows // 512)
    held = {}

    def stage_pairs(stage):
        def partner(i):
            lag, col = divmod(i, columns)
            if stage < 2:
                return lag * columns + (col ^ 1) if (lag & 1) == stage else (lag ^ 2) * columns + col
            return (lag ^ (1 << stage)) * columns + col

        return [(i, partner(i)) for i in range(owners * columns)]

    def offered(slots):
        return jnp.stack(slots[len(slots) // 2 :])

    def taken(slots, offer, stage):
        got = lax.ppermute(offer, ("lag", "col"), stage_pairs(stage))
        return [slots[i] + got[i] for i in range(len(slots) // 2)]

    def owners_sum(acc):
        for b in range(1, bits):
            half = acc.shape[0] // 2
            got = exchanged(acc[half:], "lag", 1 << b)
            if half == 1:
                return acc[0], got[0]
            acc = acc[:half] + got
        return acc[0], jnp.zeros_like(acc[0])

    def scattered(acc, bit):
        while len(acc) > 4:
            got = exchanged(jnp.stack(acc[1::2]), "col", bit)
            acc = [a + got[i] for i, a in enumerate(acc[0::2])]
            bit *= 2
        return [acc[0]] + [exchanged(acc[d], "col", d * bit) for d in range(1, len(acc))]

    def gathered(x):
        for b in reversed(range(1, bits)):
            x = jnp.concatenate([x, exchanged(x, "lag", 1 << b)], axis=0)
        return x

    def partner_sum(n):
        return held[f"keep{n}"] + exchanged(held[f"send{n}"], "lag", 1)

    def with_tail(n):
        pair = with_carried(own, held["carried"], held[f"keep{n}"], held[f"send{n}"], lag_matrices, n, owners)
        held[f"keep{n}"], held[f"send{n}"] = pair

    newest, tail = staged(own, lag_matrices, history, back)
    top = 1 << (bits - 1)
    held["newest"], held["got"] = newest, lax.ppermute(newest, "lag", [(0, top)])
    held["carried"] = lax.ppermute(tail, "lag", [(i, i + 1) for i in range(owners - 1)])
    partials = bulk(own, history, lag_matrices, steps, owners, tiles)
    for n in range(steps):
        held[f"keep{n}"], held[f"send{n}"] = partials[2 * n : 2 * n + 2]
    held["lag2"], held["lag3"] = partials[-2:]
    sealed(held, "send0", "got", "carried")

    got = exchanged(held["send0"], "lag", 1)
    slots = [held["keep0"][i] + got[i] for i in range(owners)]
    held["offer"] = offered(slots)
    sealed(held, "offer", "keep1", "newest")
    slots = taken(slots, held["offer"], 0)
    with_tail(1)
    held["field"] = whole_call(functools.partial(fields_kernel, slices=owners), "fields", [(steps, small, LANES)], own, excitation)[0]
    newest = jnp.where((owner & top) != 0, held["got"], held["newest"])
    for b in reversed(range(1, bits - 1)):
        got = lax.ppermute(newest, "lag", [(i, i + (1 << b)) for i in range(0, owners, 2 << b)])
        newest = jnp.where((owner >> b) & 1 == 1, got, newest)
    held["newest"] = newest
    held["offer"] = offered(slots)
    sealed(held, "offer", "keep1", "send1", "field", "keep2", "newest")
    held["odd"] = lax.ppermute(held["newest"], "lag", [(i, i + 1) for i in range(0, owners, 2)])
    slots = taken(slots, held["offer"], 1)
    for b in range(2, bits):
        slots = taken(slots, offered(slots), b)
    with_tail(2)
    held["past1"] = partner_sum(1)
    held["acc0"] = slots[0]
    sealed(held, "acc0", "keep2", "send2", "keep3", "odd")
    acc = whole_call(merge_kernel, "merge", [(small, LANES)] * (columns // 2), own, held["acc0"])
    parts = scattered(acc, 2)
    held["mine1"], held["got1"] = owners_sum(held["past1"])
    with_tail(3)
    held["past2"] = partner_sum(2)
    held.update((f"part{i}", part) for i, part in enumerate(parts))
    sealed(held, "keep3", "send3", "past2", "lag2", "mine1", "got1", *(f"part{i}" for i in range(len(parts))))
    a, b = held["mine1"], held["got1"]
    parts = [held[f"part{i}"] for i in range(len(parts))]

    shaped = (columns, small, LANES)
    halves = [(columns // 2, small, LANES)] * 2
    shown = []
    for n in range(1, steps):
        x, keep, send = whole_call(
            functools.partial(chain_kernel, width=width), "chain", [(small, LANES), *halves],
            own, held["field"][n - 1], a.reshape(shaped), b.reshape(shaped), held["newest"], held["odd"], *parts,
        )
        if n + 1 < steps:
            if n == 1:
                held["x"] = x
                sealed(held, "x", "lag2", "lag3", "send3")
                x = held["x"]
                held["past3"] = partner_sum(3)
                for k in (2, 3):
                    held[f"odd{k}"] = lax.ppermute(held[f"lag{k}"], "lag", [(0, 1)])
            shown.append(gathered(x[None]))
            terms = [v for k in range(2, n + 2) for v in (held[f"lag{k}"], held[f"odd{k}"], shown[n + 1 - k])]
            past = whole_call(
                functools.partial(late_kernel, width=width), "late", [held[f"past{n + 1}"].shape],
                own, held[f"past{n + 1}"], *terms,
            )[0]
            a, b = owners_sum(past)
        else:
            shown.append(gathered(x[None]))
        acc = keep + exchanged(send, "col", 1)
        parts = scattered([acc[i] for i in range(columns // 2)], 2)
    early = jnp.stack(shown, axis=1)
    early = jnp.concatenate([early, exchanged(early, "lag", 1)], axis=0)
    held["dens"] = assembled(own, early, excitation.shape, 0)
    held.update((f"part{i}", part) for i, part in enumerate(parts))
    sealed(held, "dens", *(f"part{i}" for i in range(len(parts))))
    x = held["field"][steps - 1] - functools.reduce(jnp.add, [held[f"part{i}"] for i in range(len(parts))])
    newest = gathered(x[None])
    newest = jnp.concatenate([newest, exchanged(newest, "lag", 1)], axis=0)
    return assembled(own, newest[:, None], excitation.shape, steps - 1, [held["dens"]])


def solution(mesh):
    return jax.shard_map(
        local,
        mesh=mesh,
        in_specs=(P("lag", None, "col"), P("lag", "col", None), P(None, "col", None)),
        out_specs=P(None, "col", None),
        check_vma=False,
    )
```
